512 devices in a mesh: expert: 64 (over z, x), tensor: 8 (over y, core).
Axes of the slice: x: 4, y: 4, z: 16, core: 2. Of those that a mesh axis runs over, the one named last changes fastest.
Arguments:
- tokens: bfloat16 [8192, 2048], P(('expert', 'tensor')), may hold values from -40 to 40
- cotangent: bfloat16 [8192, 2048], P(('expert', 'tensor')), may hold values from -32 to 32
- gain: float32 [2048], replicated, may hold values from 0.1 to 1.9
- expert_ids: int32 [8192, 8], P('expert'), may hold values from 0 to 127, all different within a row; in each aligned block of 128 rows (0 to 127, 128 to 255, ...) at most 12 rows name the same one
- gate_probs: float32 [8192, 8], P('expert'), may hold values from 0.05 to 0.3
- gate_up_weight: bfloat16 [512, 2048, 384], P(('expert', 'tensor')), may hold values from -0.125 to 0.125
- down_weight: bfloat16 [512, 192, 2048], P(('expert', 'tensor')), may hold values from -0.21875 to 0.21875
Outputs:
- mixed: bfloat16 [8192, 2048], P(('expert', 'tensor'))
- token_grad: bfloat16 [8192, 2048], P(('expert', 'tensor'))
- prob_grad: float32 [8192, 8], P(('expert', 'tensor'))
- gain_grad: float32 [2048], replicated
- gate_up_grad: bfloat16 [512, 2048, 384], P(('expert', 'tensor'))
- down_grad: bfloat16 [512, 192, 2048], P(('expert', 'tensor'))
The draws below stay inside these ranges and needn't reach their ends.
Inputs may be any that keep to these rules, and one draw needn't show every extreme that they name: `expert_ids`: in each aligned block of 128 rows, the tokens of one index of the expert axis, no expert is named by more than 12 rows.
All inputs are finite; a program needn't handle non-finite values.
Results may differ from the reference program's by a relative error of at most 0.009.
Values may be sent and summed in bfloat16 or wider, within the bound.
A program may use at most 128 MiB of HBM per device.

```python
import math
import jax
import jax.numpy as jnp
import numpy as np
from jax import lax

D = 2048
FF = 768
TOP = 8
TOK_GRP = 128
EXPERTS = 128
UNIT_BLOCKS = 4
FF_DEV = 192
TOKENS = 8192
CAP = 12


def draw_tokens(key, part):
    first, second, third = jax.random.split(jax.random.fold_in(key, 11), 3)
    base_draw = jax.random.truncated_normal(first, -4.0, 4.0, (TOKENS, D), jnp.float32)
    row_scale = jnp.exp(jax.random.uniform(second, (TOKENS, 1), jnp.float32, 0.0, math.log(10.0))) / math.sqrt(10.0)
    column_scale = jnp.exp(jax.random.uniform(third, (1, D), jnp.float32, 0.0, math.log(10.0))) / math.sqrt(10.0)
    return (base_draw * row_scale * column_scale).astype(jnp.bfloat16)


def draw_cotangent(key, part):
    first, second = jax.random.split(jax.random.fold_in(key, 23), 2)
    position = jnp.arange(TOKENS, dtype=jnp.float32)[:, None] / TOKENS
    roughness = jnp.exp(jax.random.uniform(second, (TOKENS, 1), jnp.float32, 0.0, math.log(2.0)))
    base_draw = jax.random.truncated_normal(first, -4.0, 4.0, (TOKENS, D), jnp.float32)
    rising = 1.0 + 2.0 * position
    return (base_draw * rising * roughness).astype(jnp.bfloat16)


def block_levels(stream_key, extent, cuts, least, top_value):
    factor_of, own = 1.0, jax.random.fold_in(stream_key, 6)
    for dim, blocks in cuts:
        heights = jnp.exp(jax.random.uniform(jax.random.fold_in(own, dim), (blocks,), jnp.float32, least / len(cuts), top_value / len(cuts)))
        factor_of = factor_of * jnp.repeat(heights, extent[dim] // blocks).reshape([-1 if axis == dim else 1 for axis in range(len(extent))])
    return factor_of


def shared_out(own_key, own, number, rows, count, top, limit, lean):
    sequence = jax.random.permutation(own_key, count)
    packed, common = load_shares(count, rows * top, limit, lean, True), load_shares(count, rows * top, limit, lean, False)
    places = jnp.arange(count)

    def named(lengths, rotation):
        used = int((lengths > 0).sum())
        fixed = max(1, used // 4)
        passed = fixed + (places - fixed + rotation * (used - fixed)) % max(1, count - fixed)
        return jnp.zeros((count,), jnp.int32).at[sequence[jnp.where(places < fixed, places, passed)]].set(jnp.asarray(lengths, jnp.int32))

    lengths = jnp.where(number % 4 == 0, named(packed, number // 4), named(common, number - number // 4 - 1))
    mixed = jax.random.permutation(jax.random.fold_in(own, 3), count)
    donor, receiver = mixed[0:count // 2 * 2:2], mixed[1:count // 2 * 2:2]
    slack = jnp.minimum(lengths[donor] - 1, limit - lengths[receiver]) // 2
    slack = jnp.where((donor == sequence[0]) | (receiver == sequence[0]) | (lengths[receiver] == 0), 0, jnp.maximum(slack, 0))
    passed = jax.random.randint(jax.random.fold_in(own, 4), (count // 2,), 0, 1 << 20) % (slack + 1)
    lengths = lengths.at[donor].add(-passed).at[receiver].add(passed)
    labels = jnp.searchsorted(jnp.cumsum(lengths), jnp.arange(rows * top), side="right").astype(jnp.int32)
    listing = labels.reshape(top, rows).T
    listing = listing[jax.random.permutation(jax.random.fold_in(own, 1), rows)]
    rotation = jax.random.randint(jax.random.fold_in(own, 2), (rows, 1), 0, top)
    return jnp.take_along_axis(listing, (jnp.arange(top)[None, :] + rotation) % top, axis=1)


def load_shares(count, total, reach, lean, full):
    weights = [(1 << 20) // math.isqrt(standing ** lean) + 1 for standing in range(1, count + 1)]
    largest = reach if full else min(reach, max(-(-total // count), total * weights[0] // sum(weights)))
    least = 1 if total - largest >= count - 1 else 0
    holding, rest = [largest] + [least] * (count - 1), total - largest - least * (count - 1)
    while rest > 0:
        free = [i for i in range(1, count) if holding[i] < largest] or [i for i in range(1, count) if holding[i] < reach]
        mass, left = sum([weights[i] for i in free]), rest
        for i in free:
            extra = min(reach - holding[i], max(1, left * weights[i] // mass), rest)
            holding[i] = holding[i] + extra
            rest = rest - extra
    return np.array(holding)


def gaussian(own_key, dims, scale, limit, cuts=(), kind=jnp.bfloat16):
    result = scale * jax.random.normal(own_key, dims, jnp.float32)
    if cuts:
        result = result * block_levels(own_key, dims, cuts, -0.22, 0.18)
    return jnp.clip(result, -limit, limit).astype(kind)


def setup_inputs(seed: int = 0) -> dict:
    streams_of = jax.random.split(jax.random.key(seed), 8)
    tokens = draw_tokens(jax.random.fold_in(streams_of[7], 71), 0)
    cotangent = draw_cotangent(jax.random.fold_in(streams_of[7], 71), 0)
    gain = jnp.clip(1.0 + 0.18 * jax.random.normal(streams_of[2], (D,), jnp.float32), 0.1, 1.9)
    expert_ids_keys = jax.random.split(jax.random.fold_in(streams_of[3], 1), TOKENS // TOK_GRP)
    expert_ids_turns = jax.random.permutation(jax.random.fold_in(streams_of[3], 3), TOKENS // TOK_GRP)
    expert_ids = jax.vmap(lambda own, number: shared_out(jax.random.fold_in(streams_of[3], 2), own, number, TOK_GRP, EXPERTS, TOP, CAP, 2))(expert_ids_keys, expert_ids_turns).reshape((TOKENS, TOP))
    gate_probs = jnp.clip(0.05 + 0.25 * jax.random.uniform(streams_of[4], (TOKENS, TOP), jnp.float32) ** block_levels(streams_of[4], (TOKENS, TOP), ((0, 64),), -0.2, 0.2), 0.05, 0.3)
    gate_up_weight = gaussian(streams_of[5], (EXPERTS * UNIT_BLOCKS, D, 2 * FF_DEV), D ** -0.5, 0.125, ((0, 512),))
    down_weight = gaussian(streams_of[6], (EXPERTS * UNIT_BLOCKS, FF_DEV, D), FF ** -0.5, 0.21875, ((0, 512),))
    return {"tokens": tokens, "cotangent": cotangent, "gain": gain, "expert_ids": expert_ids, "gate_probs": gate_probs, "gate_up_weight": gate_up_weight, "down_weight": down_weight}


def expert_forward(rows, gate_up, down_proj):
    projected = jnp.dot(rows, gate_up, preferred_element_type=jnp.float32)
    half_width = down_proj.shape[0]
    gate_pre = projected[:, :half_width]
    up_pre = projected[:, half_width:]
    sigmoid_gate = jax.nn.sigmoid(gate_pre)
    hidden = (gate_pre * sigmoid_gate * up_pre).astype(jnp.bfloat16)
    block_out = jnp.dot(hidden, down_proj, preferred_element_type=jnp.float32).astype(jnp.bfloat16)
    return (gate_pre, up_pre, sigmoid_gate, hidden, block_out)

def expert_backward(rows, slot_grads, gate_up, down_proj, gate_pre, up_pre, sigmoid_gate, hidden):
    hidden_grad = lax.dot_general(slot_grads, down_proj, (((1,), (1,)), ((), ())), preferred_element_type=jnp.float32)
    gate_grad = (hidden_grad * up_pre * sigmoid_gate * (1.0 + gate_pre * (1.0 - sigmoid_gate))).astype(jnp.bfloat16)
    up_grad = (hidden_grad * gate_pre * sigmoid_gate).astype(jnp.bfloat16)
    joined_grad = jnp.concatenate([gate_grad, up_grad], axis=1)
    down_part = lax.dot_general(hidden, slot_grads, (((0,), (0,)), ((), ())), preferred_element_type=jnp.float32).astype(jnp.bfloat16)
    gate_up_part = lax.dot_general(rows, joined_grad, (((0,), (0,)), ((), ())), preferred_element_type=jnp.float32).astype(jnp.bfloat16)
    input_grad = lax.dot_general(joined_grad, gate_up, (((1,), (1,)), ((), ())), preferred_element_type=jnp.float32).astype(jnp.bfloat16)
    return (input_grad, gate_up_part, down_part)

def reference(tokens, cotangent, gain, expert_ids, gate_probs, gate_up_weight, down_weight):
    values = tokens.astype(jnp.float32)
    inv_rms = lax.rsqrt(lax.optimization_barrier(jnp.mean(values * values, axis=1, keepdims=True)) + 1e-06)
    scaled = values * inv_rms
    normed = (scaled * gain[None, :]).astype(jnp.bfloat16)
    cot_values = cotangent.astype(jnp.float32)
    groups = TOKENS // TOK_GRP
    slots = groups * CAP
    row_ids = jnp.arange(TOKENS, dtype=jnp.int32)
    group_of = row_ids // TOK_GRP
    top_ids = jnp.arange(TOP, dtype=jnp.int32)
    normed_pad = jnp.concatenate([normed, jnp.zeros((1, D), jnp.bfloat16)], axis=0)
    cot_pad = jnp.concatenate([cot_values, jnp.zeros((1, D), jnp.float32)], axis=0)

    def per_expert(carry, expert):
        out_acc, grad_acc, prob_acc = carry
        matches = expert_ids == expert
        chosen = jnp.any(matches, axis=1)
        prob_of = lax.optimization_barrier(jnp.sum(jnp.where(matches, gate_probs, 0.0), axis=1))
        slot_of = lax.optimization_barrier(jnp.sum(jnp.where(matches, top_ids[None, :], 0), axis=1)).astype(jnp.int32)
        counts = chosen.astype(jnp.int32).reshape(groups, TOK_GRP)
        rank_in = (jnp.cumsum(counts, axis=1) - counts).reshape(TOKENS).astype(jnp.int32)
        target = jnp.where(chosen, group_of * CAP + rank_in, slots).astype(jnp.int32)
        table = jnp.full((slots + 1,), TOKENS, jnp.int32).at[target].set(row_ids)[:slots]
        rows = normed_pad[table]
        slot_cot = cot_pad[table]
        slot_prob = jnp.concatenate([prob_of, jnp.zeros((1,), prob_of.dtype)])[table]
        slot_index = jnp.concatenate([slot_of, jnp.zeros((1,), jnp.int32)])[table]
        slot_grads = (slot_prob[:, None] * slot_cot).astype(jnp.bfloat16)
        out_sum = jnp.zeros((slots, D), jnp.float32)
        input_sum = jnp.zeros((slots, D), jnp.float32)
        gate_up_parts = []
        down_parts = []
        for block_index in range(UNIT_BLOCKS):
            weight_row = (expert * UNIT_BLOCKS + block_index).astype(jnp.int32)
            gate_up = lax.dynamic_index_in_dim(gate_up_weight, weight_row, 0, keepdims=False)
            down_proj = lax.dynamic_index_in_dim(down_weight, weight_row, 0, keepdims=False)
            gate_pre, up_pre, sigmoid_gate, hidden, block_out = expert_forward(rows, gate_up, down_proj)
            input_grad, gate_up_part, down_part = expert_backward(rows, slot_grads, gate_up, down_proj, gate_pre, up_pre, sigmoid_gate, hidden)
            out_sum = out_sum + block_out.astype(jnp.float32)
            input_sum = input_sum + input_grad.astype(jnp.float32)
            gate_up_parts.append(gate_up_part)
            down_parts.append(down_part)
        out_acc = out_acc.at[table].add(slot_prob[:, None] * out_sum)
        grad_acc = grad_acc.at[table].add(input_sum)
        prob_acc = prob_acc.at[table * TOP + slot_index].add(lax.optimization_barrier(jnp.sum(slot_cot * out_sum, axis=1)))
        return ((out_acc, grad_acc, prob_acc), (jnp.stack(gate_up_parts), jnp.stack(down_parts)))
    init = (jnp.zeros((TOKENS + 1, D), jnp.float32), jnp.zeros((TOKENS + 1, D), jnp.float32), jnp.zeros(((TOKENS + 1) * TOP,), jnp.float32))
    finals, stacked = lax.scan(per_expert, init, jnp.arange(EXPERTS, dtype=jnp.int32))
    out_acc, grad_acc, prob_acc = finals
    gate_up_all, down_all = stacked
    mixed = (values + out_acc[:TOKENS]).astype(jnp.bfloat16)
    normed_grad = grad_acc[:TOKENS]
    gain_grad = lax.optimization_barrier(jnp.sum(normed_grad * scaled, axis=0))
    gain_side = normed_grad * gain[None, :]
    token_grad = (cot_values + inv_rms * (gain_side - scaled * lax.optimization_barrier(jnp.mean(gain_side * scaled, axis=1, keepdims=True)))).astype(jnp.bfloat16)
    prob_grad = prob_acc[:TOKENS * TOP].reshape(TOKENS, TOP)
    gate_up_grad = gate_up_all.reshape(EXPERTS * UNIT_BLOCKS, D, 2 * FF_DEV)
    down_grad = down_all.reshape(EXPERTS * UNIT_BLOCKS, FF_DEV, D)
    return (mixed, token_grad, prob_grad, gain_grad, gate_up_grad, down_grad)
```

```python
import functools

import jax
import jax.numpy as jnp
import numpy as np
from jax import lax
from jax.experimental import pallas as pl
from jax.experimental.pallas import tpu as pltpu
from jax.sharding import PartitionSpec as P

TOP = 8
NZ, NX, NY, NC = 16, 4, 4, 2
NT = NY * NC
TOK = 128
OWN = 16
CAP = 12
FEAT = 256
BATCH = 4
NB = NZ // BATCH
CHUNK = BATCH * CAP
ROWS = NX * CHUNK
SLOTS = NX * 2 * CHUNK
WIDE = BATCH * TOK
ORDER = [0, 1, -1, 2, -2, 3, -3, 4, -4, 5, -5, 6, -6, 7, -7, 8]
SLOT_OF = {d: s for s, d in enumerate(ORDER)}
SLOT_OF[-8] = SLOT_OF[8]
BF, F32 = jnp.bfloat16, jnp.float32


def place():
    e, t = lax.axis_index("expert"), lax.axis_index("tensor")
    return e, t, e // NX, lax.rem(e, NX), t // NC, lax.rem(t, NC)


def remote(src, dst, send, recv, device):
    return pltpu.make_async_remote_copy(
        src_ref=src, dst_ref=dst, send_sem=send, recv_sem=recv,
        device_id=device, device_id_type=pl.DeviceIdType.MESH,
    )


def greet(e, t, z, x):
    barrier = pltpu.get_barrier_semaphore()
    peers = [(e, lax.rem(t + i, NT)) for i in range(1, NT)]
    peers += [(z * NX + lax.rem(x + i, NX), t) for i in range(1, NX)]
    peers += [(lax.rem(z + i, NZ) * NX + x, t) for i in (1, NZ - 1)]
    for peer in peers:
        pl.semaphore_signal(barrier, inc=1, device_id=peer, device_id_type=pl.DeviceIdType.MESH)
    pl.semaphore_wait(barrier, len(peers))


def fill_select(codes, rmat, select):
    for f in range(2 * NX):
        hit = codes[f : f + 1, :] == rmat
        rows = pl.ds(f * CHUNK, CHUNK)
        select[0, rows, :] = jnp.where(hit, 1.0, 0.0).astype(BF)
        select[1, rows, :] = jnp.where(hit, codes[8 + f : 9 + f, :], 0.0).astype(BF)
        select[2, rows, :] = jnp.where(hit, codes[16 + f : 17 + f, :], 0.0).astype(BF)


def dispatch_kernel(
    own_ref, meta_ref, rmat_ref, tri_ref, rows_ref, codes_ref,
    zbuf, xs, yb, select,
    a_send, a_recv, z_send, z_recv, x_send, x_recv, y_send, y_recv, c_send, c_recv, local,
):
    e, t, z, x, y, c = place()
    phi = c * NY + y
    half = y // 2
    greet(e, t, z, x)
    started = []

    def feat(index):
        return pl.ds(pl.multiple_of(index * FEAT, FEAT), FEAT)

    stays = []
    for arr in range(2):
        row_at = pl.ds(pl.multiple_of(arr * TOK + t * OWN, OWN), OWN)
        for i in range(1, NT):
            other = lax.rem(t + i, NT)
            their = lax.rem(other, NC) * NY + other // NC
            n = arr * (NT - 1) + i - 1
            copy = remote(
                own_ref.at[arr, :, feat(their)], zbuf.at[0, row_at, :],
                a_send.at[n], a_recv.at[n], (e, other),
            )
            copy.start()
            started.append(copy)
        stay = pltpu.make_async_copy(own_ref.at[arr, :, feat(phi)], zbuf.at[0, row_at, :], local.at[arr])
        stay.start()
        stays.append(stay)
    zbuf[0, 2 * TOK :, :] = meta_ref[...]
    for copy in started:
        copy.wait_recv()
    for stay in stays:
        stay.wait()

    right = (lax.rem(z + 1, NZ) * NX + x, t)
    left = (lax.rem(z + NZ - 1, NZ) * NX + x, t)
    parts = (pl.ds(0, TOK), pl.ds(TOK, TOK + OWN))

    def hop(step, way):
        sign = -1 if way == 0 else 1
        src, dst = SLOT_OF[sign * (step - 1)], SLOT_OF[sign * step]
        copies = []
        for p, part in enumerate(parts):
            n = (way * 8 + step - 1) * 2 + p
            copy = remote(
                zbuf.at[src, part, :], zbuf.at[dst, part, :],
                z_send.at[n], z_recv.at[n], right if way == 0 else left,
            )
            copies.append(copy)
        return copies

    def stage_x(b):
        base = lax.convert_element_type(z * (2 * NX), F32)
        named = base + lax.broadcasted_iota(jnp.int32, (8, TOK), 0).astype(F32)
        chosen, high, low = [], [], []
        for j in range(BATCH):
            meta = zbuf[b * BATCH + j, 2 * TOK :, :].astype(F32)
            got, hi, lo = jnp.zeros((8, TOK), F32), jnp.zeros((8, TOK), F32), jnp.zeros((8, TOK), F32)
            for k in range(TOP):
                same = meta[k : k + 1, :TOK] == named
                got = got + jnp.where(same, 1.0, 0.0)
                hi = hi + jnp.where(same, meta[8 + k : 9 + k, :TOK], 0.0)
                lo = lo + jnp.where(same, meta[k : k + 1, TOK:], 0.0)
            chosen.append(got)
            high.append(hi)
            low.append(lo)
        taken = jnp.concatenate(chosen, axis=0)
        rank = jnp.dot(taken.astype(BF), tri_ref[...], preferred_element_type=F32)
        code = jnp.where(taken > 0.5, rank, -1.0)
        codes = jnp.concatenate(
            [
                jnp.concatenate([code[8 * j : 8 * j + 8] for j in range(BATCH)], axis=1),
                jnp.concatenate(high, axis=1),
                jnp.concatenate(low, axis=1),
            ],
            axis=0,
        )
        codes_ref[b] = codes
        fill_select(codes, rmat_ref[...], select)
        these = pl.ds(b * BATCH, BATCH)
        normed = zbuf[these, 0:TOK, :].reshape(WIDE, FEAT)
        cot = zbuf[these, TOK : 2 * TOK, :].reshape(WIDE, FEAT)
        picked = jnp.dot(select[0], normed, preferred_element_type=F32).astype(BF)
        grads = (
            jnp.dot(select[1], cot, preferred_element_type=F32)
            + jnp.dot(select[2], cot, preferred_element_type=F32)
        ).astype(BF)
        xs[b, :, :, 0] = picked.reshape(NX, 2, CHUNK, FEAT)
        xs[b, :, :, 1] = grads.reshape(NX, 2, CHUNK, FEAT)
        at = pl.ds(pl.multiple_of(x * CHUNK, 16), CHUNK)
        copies = []
        for i in range(1, NX):
            other = lax.rem(x + i, NX)
            n = b * (NX - 1) + i - 1
            copy = remote(
                xs.at[b, other], yb.at[b, :, :, at, :],
                x_send.at[n], x_recv.at[n], (z * NX + other, t),
            )
            copy.start()
            copies.append(copy)
        stay = pltpu.make_async_copy(xs.at[b, x], yb.at[b, :, :, at, :], local.at[2 + b])
        stay.start()
        return copies, stay

    def stage_y(b, earlier):
        copies, stay = earlier
        for copy in copies:
            copy.wait_recv()
        stay.wait()
        where = pl.ds(b * ROWS, ROWS)
        sent = []
        for i in range(1, NY):
            other = lax.rem(y + i, NY)
            n = b * (NY - 1) + i - 1
            copy = remote(
                yb.at[b, other // 2], rows_ref.at[:, where, feat(phi)],
                y_send.at[n], y_recv.at[n], (e, other * NC + c),
            )
            copy.start()
            sent.append(copy)
        keep = pltpu.make_async_copy(yb.at[b, half], rows_ref.at[:, where, feat(phi)], local.at[2 + NB + b])
        keep.start()
        return sent, keep

    def stage_c(b, earlier):
        sent, keep = earlier
        for copy in sent:
            copy.wait_recv()
        keep.wait()
        block = rows_ref.at[
            :, pl.ds(b * ROWS, ROWS), pl.ds(pl.multiple_of(c * (NY * FEAT), NY * FEAT), NY * FEAT)
        ]
        copy = remote(block, block, c_send.at[b], c_recv.at[b], (e, y * NC + 1 - c))
        copy.start()
        return copy

    flying = {}
    for way in range(2):
        flying[way] = hop(1, way)
        for copy in flying[way]:
            copy.start()
            started.append(copy)
    xdone, ydone, cdone = {}, {}, {}
    for step in range(1, 9):
        for way in range(2):
            last = 8 if way == 0 else 7
            if step > last:
                continue
            onward = hop(step + 1, way) if step < last else None
            for p in range(2):
                flying[way][p].wait_recv()
                if onward is not None:
                    onward[p].start()
                    started.append(onward[p])
            flying[way] = onward
        if step % 2 == 0:
            b = step // 2 - 1
            xdone[b] = stage_x(b)
            if b >= 1:
                ydone[b - 1] = stage_y(b - 1, xdone[b - 1])
            if b >= 2:
                cdone[b - 2] = stage_c(b - 2, ydone[b - 2])
    ydone[NB - 1] = stage_y(NB - 1, xdone[NB - 1])
    cdone[NB - 2] = stage_c(NB - 2, ydone[NB - 2])
    cdone[NB - 1] = stage_c(NB - 1, ydone[NB - 1])
    for b in range(NB):
        cdone[b].wait_recv()
    for copy in started:
        copy.wait_send()
    for b in range(NB):
        for copy in xdone[b][0] + ydone[b][0] + [cdone[b]]:
            copy.wait_send()


def return_kernel(
    parts_ref, codes_ref, rmat_ref, out_ref,
    cb, ys, yr, q, xb, dense, ring_out, ring_in, total, select,
    c_send, c_recv, y_send, y_recv, x_send, x_recv, z_send, z_recv, a_send, a_recv, local,
):
    e, t, z, x, y, c = place()
    phi = c * NY + y
    half = y // 2
    greet(e, t, z, x)
    started = []
    order = list(range(NB - 1, -1, -1))

    core = {}
    for b in order:
        copy = remote(
            parts_ref.at[
                :, pl.ds(b * ROWS, ROWS),
                pl.ds(pl.multiple_of((1 - c) * (NY * FEAT), NY * FEAT), NY * FEAT),
            ],
            cb.at[b], c_send.at[b], c_recv.at[b], (e, y * NC + 1 - c),
        )
        copy.start()
        core[b] = copy
        started.append(copy)

    def stage_y(b):
        core[b].wait_recv()
        for k in range(NY):
            mine = parts_ref[
                :, pl.ds(b * ROWS, ROWS), pl.ds(pl.multiple_of((c * NY + k) * FEAT, FEAT), FEAT)
            ]
            theirs = cb[b, :, :, k * FEAT : (k + 1) * FEAT]
            ys[b, k] = (mine.astype(F32) + theirs.astype(F32)).astype(BF)
        sent = []
        for i in range(1, NY):
            other = lax.rem(y + i, NY)
            n = b * (NY - 1) + i - 1
            copy = remote(
                ys.at[b, other], yr.at[b, i - 1], y_send.at[n], y_recv.at[n], (e, other * NC + c)
            )
            copy.start()
            sent.append(copy)
            started.append(copy)
        return sent

    def stage_x(b, sent):
        for copy in sent:
            copy.wait_recv()
        odd = lax.rem(y, 2)
        partner = 2 * (1 - odd)
        q[b, half] = (ys[b, y].astype(F32) + yr[b, partner].astype(F32)).astype(BF)
        q[b, 1 - half] = (yr[b, 1].astype(F32) + yr[b, 2 * odd].astype(F32)).astype(BF)
        copies = []
        for i in range(1, NX):
            other = lax.rem(x + i, NX)
            n = b * (NX - 1) + i - 1
            copy = remote(
                q.at[b, :, :, pl.ds(pl.multiple_of(other * CHUNK, 16), CHUNK), :], xb.at[b, x],
                x_send.at[n], x_recv.at[n], (z * NX + other, t),
            )
            copy.start()
            copies.append(copy)
            started.append(copy)
        stay = pltpu.make_async_copy(
            q.at[b, :, :, pl.ds(pl.multiple_of(x * CHUNK, 16), CHUNK), :], xb.at[b, x], local.at[b]
        )
        stay.start()
        return copies, stay

    def spread(b, earlier):
        copies, stay = earlier
        fill_select(codes_ref[b], rmat_ref[...], select)
        for copy in copies:
            copy.wait_recv()
        stay.wait()
        over = (((0,), (0,)), ((), ()))
        outs = xb[b, :, :, 0].reshape(SLOTS, FEAT)
        grads = xb[b, :, :, 1].reshape(SLOTS, FEAT)
        first = lax.dot_general(select[1], outs, over, preferred_element_type=F32)
        first = first + lax.dot_general(select[2], outs, over, preferred_element_type=F32)
        second = lax.dot_general(select[0], grads, over, preferred_element_type=F32)
        for j in range(BATCH):
            dense[b * BATCH + j, 0] = first[j * TOK : (j + 1) * TOK]
            dense[b * BATCH + j, 1] = second[j * TOK : (j + 1) * TOK]

    right = (lax.rem(z + 1, NZ) * NX + x, t)
    left = (lax.rem(z + NZ - 1, NZ) * NX + x, t)
    ring = {}

    def hop(step, way):
        n = way * 8 + step
        slot = SLOT_OF[8 - step] if way == 0 else SLOT_OF[-(7 - step)]
        for arr in range(2):
            value = dense[slot, arr]
            if step > 0:
                ring[way, step - 1, arr].wait_recv()
                value = value + ring_in[n - 1, arr].astype(F32)
            ring_out[n, arr] = value.astype(BF)
            copy = remote(
                ring_out.at[n, arr], ring_in.at[n, arr], z_send.at[2 * n + arr], z_recv.at[2 * n + arr],
                right if way == 0 else left,
            )
            copy.start()
            ring[way, step, arr] = copy
            started.append(copy)

    ysent, xsent = {}, {}
    for b in order:
        ysent[b] = stage_y(b)
    xsent[3] = stage_x(3, ysent[3])
    for n, b in enumerate(order):
        if b > 0:
            xsent[b - 1] = stage_x(b - 1, ysent[b - 1])
        spread(b, xsent[b])
        for step in (2 * n, 2 * n + 1):
            hop(step, 0)
            if step < 7:
                hop(step, 1)
    finals = []
    for arr in range(2):
        ring[0, 7, arr].wait_recv()
        ring[1, 6, arr].wait_recv()
        total[arr] = dense[0, arr] + ring_in[7, arr].astype(F32) + ring_in[8 + 6, arr].astype(F32)
        spot = pl.ds(pl.multiple_of(phi * FEAT, FEAT), FEAT)
        for i in range(1, NT):
            other = lax.rem(t + i, NT)
            n = arr * (NT - 1) + i - 1
            copy = remote(
                total.at[arr, pl.ds(pl.multiple_of(other * OWN, OWN), OWN), :], out_ref.at[arr, :, spot],
                a_send.at[n], a_recv.at[n], (e, other),
            )
            copy.start()
            finals.append(copy)
        stay = pltpu.make_async_copy(
            total.at[arr, pl.ds(pl.multiple_of(t * OWN, OWN), OWN), :], out_ref.at[arr, :, spot],
            local.at[NB + arr],
        )
        stay.start()
        stay.wait()
    for copy in finals:
        copy.wait_recv()
    for copy in started + finals:
        copy.wait_send()


def vmem():
    return pl.BlockSpec(memory_space=pltpu.VMEM)


def dma(*counts):
    return [pltpu.SemaphoreType.DMA((n,)) for n in counts for _ in range(2)]


def constants():
    lane = np.arange(WIDE)
    row = np.arange(CHUNK)
    rmat = np.where(lane[None, :] // TOK == row[:, None] // CAP, row[:, None] % CAP, -5)
    tri = np.arange(TOK)[:, None] < np.arange(TOK)[None, :]
    return jnp.asarray(rmat, F32), jnp.asarray(tri, BF)


def dispatch(own, meta, rmat, tri):
    width = NT * FEAT
    return pl.pallas_call(
        dispatch_kernel,
        out_shape=(
            jax.ShapeDtypeStruct((2, NB * ROWS, width), BF),
            jax.ShapeDtypeStruct((NB, 24, WIDE), F32),
        ),
        in_specs=[vmem()] * 4,
        out_specs=(vmem(), vmem()),
        scratch_shapes=[
            pltpu.VMEM((NZ, 2 * TOK + OWN, FEAT), BF),
            pltpu.VMEM((NB, NX, 2, 2, CHUNK, FEAT), BF),
            pltpu.VMEM((NB, 2, 2, ROWS, FEAT), BF),
            pltpu.VMEM((3, SLOTS, WIDE), BF),
            *dma(2 * (NT - 1), 32, NB * (NX - 1), NB * (NY - 1), NB),
            pltpu.SemaphoreType.DMA((2 + 2 * NB,)),
        ],
        compiler_params=pltpu.CompilerParams(
            collective_id=0, has_side_effects=True, vmem_limit_bytes=48 * 2**20
        ),
        name="dispatch",
    )(own, meta, rmat, tri)


def give_back(parts, codes, rmat):
    width = NT * FEAT
    return pl.pallas_call(
        return_kernel,
        out_shape=jax.ShapeDtypeStruct((2, OWN, width), F32),
        in_specs=[vmem()] * 3,
        out_specs=vmem(),
        scratch_shapes=[
            pltpu.VMEM((NB, 2, ROWS, NY * FEAT), BF),
            pltpu.VMEM((NB, NY, 2, ROWS, FEAT), BF),
            pltpu.VMEM((NB, NY - 1, 2, ROWS, FEAT), BF),
            pltpu.VMEM((NB, 2, 2, ROWS, FEAT), BF),
            pltpu.VMEM((NB, NX, 2, 2, CHUNK, FEAT), BF),
            pltpu.VMEM((NZ, 2, TOK, FEAT), F32),
            pltpu.VMEM((NZ, 2, TOK, FEAT), BF),
            pltpu.VMEM((NZ, 2, TOK, FEAT), BF),
            pltpu.VMEM((2, TOK, FEAT), F32),
            pltpu.VMEM((3, SLOTS, WIDE), BF),
            *dma(NB, NB * (NY - 1), NB * (NX - 1), 32, 2 * (NT - 1)),
            pltpu.SemaphoreType.DMA((NB + 2,)),
        ],
        compiler_params=pltpu.CompilerParams(
            collective_id=1, has_side_effects=True, vmem_limit_bytes=56 * 2**20
        ),
        name="give_back",
    )(parts, codes, rmat)


def shards(tokens, cotangent, gain, expert_ids, gate_probs, gate_up_weight, down_weight):
    z = lax.axis_index("expert") // NX
    t = lax.axis_index("tensor")
    values = tokens.astype(F32)
    inv_rms = lax.rsqrt(jnp.mean(values * values, axis=1, keepdims=True) + 1e-06)
    scaled = values * inv_rms
    normed = (scaled * gain[None, :]).astype(BF)
    own = jnp.stack([normed, cotangent])
    probs_t = gate_probs.T
    high = probs_t.astype(BF)
    low = (probs_t - high.astype(F32)).astype(BF)
    meta = jnp.concatenate(
        [
            jnp.concatenate([expert_ids.T.astype(BF), high], axis=0),
            jnp.concatenate([low, jnp.zeros_like(low)], axis=0),
        ],
        axis=1,
    )
    rmat, tri = constants()
    routed, codes = dispatch(own, meta, rmat, tri)
    rows, slot_grads = routed[0], routed[1]

    gate_up, down_proj = gate_up_weight[0], down_weight[0]
    width = down_proj.shape[0]
    projected = jnp.dot(rows, gate_up, preferred_element_type=F32)
    gate_pre, up_pre = projected[:, :width], projected[:, width:]
    sig = jax.nn.sigmoid(gate_pre)
    hidden = (gate_pre * sig * up_pre).astype(BF)
    block_out = jnp.dot(hidden, down_proj, preferred_element_type=F32).astype(BF)
    hidden_grad = lax.dot_general(slot_grads, down_proj, (((1,), (1,)), ((), ())), preferred_element_type=F32)
    prob_slots = jnp.sum(hidden_grad * hidden.astype(F32), axis=1)
    joined = jnp.concatenate(
        [
            (hidden_grad * up_pre * sig * (1.0 + gate_pre * (1.0 - sig))).astype(BF),
            (hidden_grad * gate_pre * sig).astype(BF),
        ],
        axis=1,
    )
    over_rows = (((0,), (0,)), ((), ()))
    input_grad = lax.dot_general(joined, gate_up, (((1,), (1,)), ((), ())), preferred_element_type=F32).astype(BF)
    summed = give_back(jnp.stack([block_out, input_grad]), codes, rmat)
    down_grad = lax.dot_general(hidden, slot_grads, over_rows, preferred_element_type=F32).astype(BF)
    gate_up_sum = lax.dot_general(rows, joined, over_rows, preferred_element_type=F32)
    gate_up_grad = gate_up_sum.astype(BF)

    gain_part = jnp.sum(gate_up.astype(F32) * gate_up_sum, axis=1)
    gain_grad = lax.psum(gain_part, ("expert", "tensor")) / gain

    by_slot = prob_slots.reshape(NB, NX, BATCH, CAP).transpose(0, 2, 1, 3).reshape(NZ, NX * CAP)
    slots = [SLOT_OF[(d + 7) % NZ - 7] for d in range(NZ)]
    by_distance = jnp.concatenate([by_slot[s : s + 1] for s in slots * 2], axis=0)
    by_group = lax.dynamic_slice_in_dim(by_distance, lax.rem(NZ - z, NZ), NZ, axis=0).reshape(NZ * NX, CAP)
    home = lax.all_to_all(by_group, "expert", split_axis=0, concat_axis=0, tiled=True)
    kind = t // NY
    targets = jnp.arange(NZ * NX, dtype=jnp.int32) * 2 + kind
    matches = expert_ids[:, :, None] == targets[None, None, :]
    chosen = jnp.any(matches, axis=1)
    earlier = jnp.arange(TOK)[None, :] < jnp.arange(TOK)[:, None]
    rank = jnp.dot(earlier.astype(BF), chosen.astype(BF), preferred_element_type=F32).astype(jnp.int32)
    picked = rank[:, :, None] == jnp.arange(CAP, dtype=jnp.int32)[None, None, :]
    value = jnp.sum(jnp.where(picked, home[None, :, :], 0.0), axis=2)
    prob_part = jnp.sum(jnp.where(matches, value[:, None, :], 0.0), axis=2)
    prob_sum = lax.psum_scatter(prob_part, "tensor", scatter_dimension=0, tiled=True)
    prob_grad = prob_sum / lax.dynamic_slice_in_dim(gate_probs, t * OWN, OWN, axis=0)

    mixed = (values + summed[0]).astype(BF)
    gain_side = summed[1] * gain[None, :]
    token_grad = (
        cotangent.astype(F32)
        + inv_rms * (gain_side - scaled * jnp.mean(gain_side * scaled, axis=1, keepdims=True))
    ).astype(BF)
    return (mixed, token_grad, prob_grad, gain_grad, gate_up_grad[None], down_grad[None])


def solution(mesh):
    both = P(("expert", "tensor"), None)
    cube = P(("expert", "tensor"), None, None)
    in_specs = (both, both, P(), P("expert", None), P("expert", None), cube, cube)
    out_specs = (both, both, both, P(), cube, cube)
    return jax.shard_map(shards, mesh=mesh, in_specs=in_specs, out_specs=out_specs, check_vma=False)
```

```python
import jax
import jax.numpy as jnp
import numpy as np
from jax import lax
from jax.experimental import pallas as pl
from jax.experimental.pallas import tpu as pltpu
from jax.sharding import PartitionSpec as P

TOP = 8
NZ, NX, NY, NC = 16, 4, 4, 2
NT = NY * NC
TOK = 128
OWN = 16
CAP = 12
FEAT = 256
BATCH = 4
NB = NZ // BATCH
CHUNK = BATCH * CAP
ROWS = NX * CHUNK
SLOTS = NX * 2 * CHUNK
WIDE = BATCH * TOK
ORDER = [0, 1, -1, 2, -2, 3, -3, 4, -4, 5, -5, 6, -6, 7, -7, 8]
SLOT_OF = {d: s for s, d in enumerate(ORDER)}
SLOT_OF[-8] = SLOT_OF[8]
BF, F32 = jnp.bfloat16, jnp.float32
ACROSS = (((1,), (1,)), ((), ()))
OVER = (((0,), (0,)), ((), ()))


def place():
    e, t = lax.axis_index("expert"), lax.axis_index("tensor")
    return e, t, e // NX, lax.rem(e, NX), t // NC, lax.rem(t, NC)


def remote(src, dst, send, recv, device):
    return pltpu.make_async_remote_copy(
        src_ref=src, dst_ref=dst, send_sem=send, recv_sem=recv,
        device_id=device, device_id_type=pl.DeviceIdType.MESH,
    )


def greet(e, t, z, x):
    barrier = pltpu.get_barrier_semaphore()
    peers = [(e, lax.rem(t + i, NT)) for i in range(1, NT)]
    peers += [(z * NX + lax.rem(x + i, NX), t) for i in range(1, NX)]
    peers += [(lax.rem(z + i, NZ) * NX + x, t) for i in (1, NZ - 1)]
    for peer in peers:
        pl.semaphore_signal(barrier, inc=1, device_id=peer, device_id_type=pl.DeviceIdType.MESH)
    pl.semaphore_wait(barrier, len(peers))


def experts_kernel(
    normed_ref, cot_ref, meta_ref, rmat_ref, tri_ref, up_ref, down_ref,
    out_ref, prob_ref, gain_ref, up_grad_ref, down_grad_ref,
    zbuf, xs, yb, select, routed, parts, hid, joined,
    cb, ys, yr, q, xb, dense, ring_out, ring_in, total,
    pdense, pring_out, pring_in, ptotal, pgot, gsend, gone, gx, gz,
    a_send, a_recv, z_send, z_recv, x_send, x_recv, y_send, y_recv, c_send, c_recv,
    c2_send, c2_recv, y2_send, y2_recv, x2_send, x2_recv, z2_send, z2_recv, a2_send, a2_recv,
    p_send, p_recv, pa_send, pa_recv, g1_send, g1_recv, g2_send, g2_recv, g3_send, g3_recv,
    g4_send, g4_recv, local,
):
    e, t, z, x, y, c = place()
    phi = c * NY + y
    half = y // 2
    width = hid.shape[1]
    greet(e, t, z, x)
    started = []

    def feat(index):
        return pl.ds(pl.multiple_of(index * FEAT, FEAT), FEAT)

    def core_half(index):
        return pl.ds(pl.multiple_of(index * (NY * FEAT), NY * FEAT), NY * FEAT)

    def block16(index, size):
        return pl.ds(pl.multiple_of(index * size, 16), size)

    def go(src, dst, send, recv, n, device):
        copy = remote(src, dst, send.at[n], recv.at[n], device)
        copy.start()
        started.append(copy)
        return copy

    def others():
        return [(i, lax.rem(t + i, NT)) for i in range(1, NT)]

    def phi_of(other):
        return lax.rem(other, NC) * NY + other // NC

    right = (lax.rem(z + 1, NZ) * NX + x, t)
    left = (lax.rem(z + NZ - 1, NZ) * NX + x, t)

    stays = []
    arrivals = []
    for arr, ref in enumerate((normed_ref, cot_ref)):
        row_at = block16(arr * (TOK // OWN) + t, OWN)
        for i, other in others():
            n = arr * (NT - 1) + i - 1
            arrivals.append(
                go(ref.at[:, feat(phi_of(other))], zbuf.at[0, row_at, :], a_send, a_recv, n, (e, other))
            )
        stay = pltpu.make_async_copy(ref.at[:, feat(phi)], zbuf.at[0, row_at, :], local.at[arr])
        stay.start()
        stays.append(stay)
    zbuf[0, 2 * TOK :, :] = meta_ref[...]
    for copy in arrivals:
        copy.wait_recv()
    for stay in stays:
        stay.wait()

    pieces = (pl.ds(0, TOK), pl.ds(TOK, TOK + OWN))

    def hop(step, way, p):
        sign = -1 if way == 0 else 1
        src, dst = SLOT_OF[sign * (step - 1)], SLOT_OF[sign * step]
        return go(
            zbuf.at[src, pieces[p], :], zbuf.at[dst, pieces[p], :], z_send, z_recv,
            (way * 8 + step - 1) * 2 + p, right if way == 0 else left,
        )

    def named_experts():
        base = lax.convert_element_type(z * (2 * NX), F32)
        return base + lax.broadcasted_iota(jnp.int32, (8, TOK), 0).astype(F32)

    def stage_x(b):
        named = named_experts()
        chosen, high, low = [], [], []
        for j in range(BATCH):
            meta = zbuf[b * BATCH + j, 2 * TOK :, :].astype(F32)
            got, hi, lo = jnp.zeros((8, TOK), F32), jnp.zeros((8, TOK), F32), jnp.zeros((8, TOK), F32)
            for k in range(TOP):
                same = meta[k : k + 1, :TOK] == named
                got = got + jnp.where(same, 1.0, 0.0)
                hi = hi + jnp.where(same, meta[8 + k : 9 + k, :TOK], 0.0)
                lo = lo + jnp.where(same, meta[k : k + 1, TOK:], 0.0)
            chosen.append(got)
            high.append(hi)
            low.append(lo)
        taken = jnp.concatenate(chosen, axis=0)
        rank = jnp.dot(taken.astype(BF), tri_ref[...], preferred_element_type=F32)
        code = jnp.where(taken > 0.5, rank, -1.0)
        codes = jnp.concatenate(
            [
                jnp.concatenate([code[8 * j : 8 * j + 8] for j in range(BATCH)], axis=1),
                jnp.concatenate(high, axis=1),
                jnp.concatenate(low, axis=1),
            ],
            axis=0,
        )
        for f in range(2 * NX):
            hit = codes[f : f + 1, :] == rmat_ref[...]
            rows = pl.ds(f * CHUNK, CHUNK)
            select[b, 0, rows, :] = jnp.where(hit, 1.0, 0.0).astype(BF)
            select[b, 1, rows, :] = jnp.where(hit, codes[8 + f : 9 + f, :], 0.0).astype(BF)
            select[b, 2, rows, :] = jnp.where(hit, codes[16 + f : 17 + f, :], 0.0).astype(BF)
        these = pl.ds(b * BATCH, BATCH)
        normed = zbuf[these, 0:TOK, :].reshape(WIDE, FEAT)
        cot = zbuf[these, TOK : 2 * TOK, :].reshape(WIDE, FEAT)
        picked = jnp.dot(select[b, 0], normed, preferred_element_type=F32).astype(BF)
        grads = (
            jnp.dot(select[b, 1], cot, preferred_element_type=F32)
            + jnp.dot(select[b, 2], cot, preferred_element_type=F32)
        ).astype(BF)
        xs[b, :, :, 0] = picked.reshape(NX, 2, CHUNK, FEAT)
        xs[b, :, :, 1] = grads.reshape(NX, 2, CHUNK, FEAT)
        at = block16(x, CHUNK)
        copies = []
        for i in range(1, NX):
            other = lax.rem(x + i, NX)
            copies.append(
                go(
                    xs.at[b, other], yb.at[b, :, :, at, :], x_send, x_recv,
                    b * (NX - 1) + i - 1, (z * NX + other, t),
                )
            )
        stay = pltpu.make_async_copy(xs.at[b, x], yb.at[b, :, :, at, :], local.at[2 + b])
        stay.start()
        return copies, stay

    def stage_y(b, earlier):
        copies, stay = earlier
        for copy in copies:
            copy.wait_recv()
        stay.wait()
        where = pl.ds(b * ROWS, ROWS)
        sent = []
        for i in range(1, NY):
            other = lax.rem(y + i, NY)
            sent.append(
                go(
                    yb.at[b, other // 2], routed.at[:, where, feat(phi)], y_send, y_recv,
                    b * (NY - 1) + i - 1, (e, other * NC + c),
                )
            )
        keep = pltpu.make_async_copy(yb.at[b, half], routed.at[:, where, feat(phi)], local.at[2 + NB + b])
        keep.start()
        return sent, keep

    def stage_c(b, earlier):
        sent, keep = earlier
        for copy in sent:
            copy.wait_recv()
        keep.wait()
        block = routed.at[:, pl.ds(b * ROWS, ROWS), core_half(c)]
        return go(block, block, c_send, c_recv, b, (e, y * NC + 1 - c))

    def compute(b, earlier):
        earlier.wait_recv()
        where = pl.ds(b * ROWS, ROWS)
        projected = jnp.dot(routed[0, where, :], up_ref[...], preferred_element_type=F32)
        gate_pre, up_pre = projected[:, :width], projected[:, width:]
        sig = jax.nn.sigmoid(gate_pre)
        hidden = (gate_pre * sig * up_pre).astype(BF)
        hid[where, :] = hidden
        hidden_grad = lax.dot_general(routed[1, where, :], down_ref[...], ACROSS, preferred_element_type=F32)
        both = jnp.concatenate(
            [
                hidden_grad * up_pre * sig * (1.0 + gate_pre * (1.0 - sig)),
                hidden_grad * gate_pre * sig,
            ],
            axis=1,
        ).astype(BF)
        joined[where, :] = both
        for n in range(4):
            cols = pl.ds(n * 2 * FEAT, 2 * FEAT)
            parts[0, where, cols] = jnp.dot(hidden, down_ref[:, cols], preferred_element_type=F32).astype(BF)
            parts[1, where, cols] = lax.dot_general(
                both, up_ref[cols, :], ACROSS, preferred_element_type=F32
            ).astype(BF)
        return go(parts.at[:, where, core_half(1 - c)], cb.at[b], c2_send, c2_recv, b, (e, y * NC + 1 - c))

    def weight_grads():
        for n in range(4):
            cols = pl.ds(n * 2 * FEAT, 2 * FEAT)
            down_grad_ref[:, cols] = lax.dot_general(
                hid[...], routed[1, :, cols], OVER, preferred_element_type=F32
            ).astype(BF)
            grad = lax.dot_general(routed[0, :, cols], joined[...], OVER, preferred_element_type=F32)
            up_grad_ref[cols, :] = grad.astype(BF)
            summed = lax.dot_general(
                jnp.ones((8, 2 * width), F32), grad * up_ref[cols, :].astype(F32), ACROSS,
                precision=lax.Precision.HIGHEST, preferred_element_type=F32,
            )
            gsend[2 * n] = summed[:, :FEAT]
            gsend[2 * n + 1] = summed[:, FEAT:]

    def back_y(b, earlier):
        earlier.wait_recv()
        for k in range(NY):
            mine = parts[:, pl.ds(b * ROWS, ROWS), feat(c * NY + k)]
            theirs = cb[b, :, :, k * FEAT : (k + 1) * FEAT]
            ys[b, k] = (mine.astype(F32) + theirs.astype(F32)).astype(BF)
        sent = []
        for i in range(1, NY):
            other = lax.rem(y + i, NY)
            sent.append(
                go(
                    ys.at[b, other], yr.at[b, i - 1], y2_send, y2_recv,
                    b * (NY - 1) + i - 1, (e, other * NC + c),
                )
            )
        return sent

    def back_x(b, sent):
        for copy in sent:
            copy.wait_recv()
        odd = lax.rem(y, 2)
        partner = 2 * (1 - odd)
        q[b, half] = (ys[b, y].astype(F32) + yr[b, partner].astype(F32)).astype(BF)
        q[b, 1 - half] = (yr[b, 1].astype(F32) + yr[b, 2 * odd].astype(F32)).astype(BF)
        copies = []
        for i in range(1, NX):
            other = lax.rem(x + i, NX)
            copies.append(
                go(
                    q.at[b, :, :, block16(other, CHUNK), :], xb.at[b, x], x2_send, x2_recv,
                    b * (NX - 1) + i - 1, (z * NX + other, t),
                )
            )
        stay = pltpu.make_async_copy(
            q.at[b, :, :, block16(x, CHUNK), :], xb.at[b, x], local.at[2 + 2 * NB + b]
        )
        stay.start()
        return copies, stay

    def spread(b, earlier):
        copies, stay = earlier
        these = pl.ds(b * BATCH, BATCH)
        cot = zbuf[these, TOK : 2 * TOK, :].reshape(WIDE, FEAT)
        cot_slots = jnp.dot(select[b, 0], cot, preferred_element_type=F32)
        for copy in copies:
            copy.wait_recv()
        stay.wait()
        outs = xb[b, :, :, 0].reshape(SLOTS, FEAT)
        grads = xb[b, :, :, 1].reshape(SLOTS, FEAT)
        first = lax.dot_general(select[b, 1], outs, OVER, preferred_element_type=F32)
        first = first + lax.dot_general(select[b, 2], outs, OVER, preferred_element_type=F32)
        second = lax.dot_general(select[b, 0], grads, OVER, preferred_element_type=F32)
        for j in range(BATCH):
            dense[b * BATCH + j, 0] = first[j * TOK : (j + 1) * TOK]
            dense[b * BATCH + j, 1] = second[j * TOK : (j + 1) * TOK]
        value = jnp.sum(cot_slots * outs.astype(F32), axis=1, keepdims=True)
        by_expert = jnp.concatenate(
            [
                jnp.sum(
                    select[b, 0, f * CHUNK : (f + 1) * CHUNK, :].astype(F32)
                    * value[f * CHUNK : (f + 1) * CHUNK],
                    axis=0, keepdims=True,
                )
                for f in range(2 * NX)
            ],
            axis=0,
        )
        named = named_experts()
        for j in range(BATCH):
            ids = zbuf[b * BATCH + j, 2 * TOK :, :TOK].astype(F32)
            mine = by_expert[:, j * TOK : (j + 1) * TOK]
            pdense[b * BATCH + j] = jnp.concatenate(
                [
                    jnp.sum(jnp.where(ids[k : k + 1] == named, mine, 0.0), axis=0, keepdims=True)
                    for k in range(TOP)
                ],
                axis=0,
            )

    ring = {}

    def back_hop(step, way):
        n = way * 8 + step
        slot = SLOT_OF[8 - step] if way == 0 else SLOT_OF[-(7 - step)]
        device = right if way == 0 else left
        for arr in range(2):
            value = dense[slot, arr]
            if step > 0:
                ring[way, step - 1, arr].wait_recv()
                value = value + ring_in[n - 1, arr].astype(F32)
            ring_out[n, arr] = value.astype(BF)
            ring[way, step, arr] = go(
                ring_out.at[n, arr], ring_in.at[n, arr], z2_send, z2_recv, 2 * n + arr, device
            )
        value = pdense[slot]
        if step > 0:
            ring[way, step - 1, 2].wait_recv()
            ring[way, step - 1, 3].wait_recv()
            value = value + pring_in[n - 1]
        pring_out[n] = value
        ring[way, step, 2] = go(pring_out.at[n], pring_in.at[n], p_send, p_recv, n, device)
        origin = lax.rem(z - step + NZ, NZ) if way == 0 else lax.rem(z + step, NZ)
        ring[way, step, 3] = go(gz.at[origin], gz.at[origin], g3_send, g3_recv, n, device)

    flying = {}
    for p in range(2):
        for way in range(2):
            flying[way, p] = hop(1, way, p)
    xdone, ydone, cdone, back = {}, {}, {}, {}
    for step in range(1, 9):
        for p in range(2):
            for way in range(2):
                last = 8 if way == 0 else 7
                if step > last:
                    continue
                flying[way, p].wait_recv()
                if step < last:
                    flying[way, p] = hop(step + 1, way, p)
        if step % 2 == 0:
            b = step // 2 - 1
            xdone[b] = stage_x(b)
            if b >= 1:
                ydone[b - 1] = stage_y(b - 1, xdone[b - 1])
            if b >= 2:
                cdone[b - 2] = stage_c(b - 2, ydone[b - 2])
    ydone[3] = stage_y(3, xdone[3])
    back[0] = compute(0, cdone[0])
    cdone[2] = stage_c(2, ydone[2])
    back[1] = compute(1, cdone[1])
    back[2] = compute(2, cdone[2])
    cdone[3] = stage_c(3, ydone[3])
    back[3] = compute(3, cdone[3])

    ysent = {}
    for b in (3, 2, 1, 0):
        ysent[b] = back_y(b, back[b])
    weight_grads()
    gains = []
    for i, other in others():
        their = phi_of(other)
        gains.append(go(gsend.at[their], gone.at[i], g1_send, g1_recv, i - 1, (e, other)))
    gone[0] = gsend[phi]
    xsent = back_x(3, ysent[3])
    for copy in gains:
        copy.wait_recv()
    gain_sum = gone[0]
    for i in range(1, NT):
        gain_sum = gain_sum + gone[i]
    gx[x] = gain_sum
    gains = []
    for i in range(1, NX):
        other = lax.rem(x + i, NX)
        gains.append(go(gx.at[x], gx.at[x], g2_send, g2_recv, i - 1, (z * NX + other, t)))
    for copy in gains:
        copy.wait_recv()
    gz[z] = gx[0] + gx[1] + gx[2] + gx[3]
    for n, b in enumerate((3, 2, 1, 0)):
        if n > 0:
            xsent = back_x(b, ysent[b])
        spread(b, xsent)
        for step in (2 * n, 2 * n + 1):
            back_hop(step, 0)
            if step < 7:
                back_hop(step, 1)

    finals = []
    for arr in range(2):
        ring[0, 7, arr].wait_recv()
        ring[1, 6, arr].wait_recv()
        total[arr] = dense[0, arr] + ring_in[7, arr].astype(F32) + ring_in[8 + 6, arr].astype(F32)
        for i, other in others():
            n = arr * (NT - 1) + i - 1
            finals.append(
                go(
                    total.at[arr, block16(other, OWN), :], out_ref.at[arr, :, feat(phi)],
                    a2_send, a2_recv, n, (e, other),
                )
            )
        stay = pltpu.make_async_copy(
            total.at[arr, block16(t, OWN), :], out_ref.at[arr, :, feat(phi)], local.at[arr]
        )
        stay.start()
        stays.append(stay)
    for way in range(2):
        for kind in (2, 3):
            ring[way, 7 - way, kind].wait_recv()
    ptotal[...] = pdense[0] + pring_in[7] + pring_in[8 + 6]
    gain_sum = gz[0]
    for n in range(1, NZ):
        gain_sum = gain_sum + gz[n]
    gain_ref[phi] = gain_sum
    for i, other in others():
        finals.append(go(ptotal, pgot.at[i - 1], pa_send, pa_recv, i - 1, (e, other)))
        finals.append(go(gain_ref.at[phi], gain_ref.at[phi], g4_send, g4_recv, i - 1, (e, other)))
    for copy in finals:
        copy.wait_recv()
    for stay in stays[2:]:
        stay.wait()
    prob_sum = ptotal[...]
    for i in range(NT - 1):
        prob_sum = prob_sum + pgot[i]
    prob_ref[...] = prob_sum
    for copy in started:
        copy.wait_send()


def vmem():
    return pl.BlockSpec(memory_space=pltpu.VMEM)


def dma(*counts):
    return [pltpu.SemaphoreType.DMA((n,)) for n in counts for _ in range(2)]


def constants():
    lane = np.arange(WIDE)
    row = np.arange(CHUNK)
    rmat = np.where(lane[None, :] // TOK == row[:, None] // CAP, row[:, None] % CAP, -5)
    tri = np.arange(TOK)[:, None] < np.arange(TOK)[None, :]
    return jnp.asarray(rmat, F32), jnp.asarray(tri, BF)


def experts(normed, cotangent, meta, gate_up, down_proj):
    features, hidden = NT * FEAT, down_proj.shape[0]
    rows = NB * ROWS
    shape = jax.ShapeDtypeStruct
    rmat, tri = constants()
    return pl.pallas_call(
        experts_kernel,
        out_shape=(
            shape((2, OWN, features), F32),
            shape((TOP, TOK), F32),
            shape((NT, 8, FEAT), F32),
            shape((features, 2 * hidden), BF),
            shape((hidden, features), BF),
        ),
        in_specs=[vmem()] * 7,
        out_specs=tuple([vmem()] * 5),
        scratch_shapes=[
            pltpu.VMEM((NZ, 2 * TOK + OWN, FEAT), BF),
            pltpu.VMEM((NB, NX, 2, 2, CHUNK, FEAT), BF),
            pltpu.VMEM((NB, 2, 2, ROWS, FEAT), BF),
            pltpu.VMEM((NB, 3, SLOTS, WIDE), BF),
            pltpu.VMEM((2, rows, features), BF),
            pltpu.VMEM((2, rows, features), BF),
            pltpu.VMEM((rows, hidden), BF),
            pltpu.VMEM((rows, 2 * hidden), BF),
            pltpu.VMEM((NB, 2, ROWS, NY * FEAT), BF),
            pltpu.VMEM((NB, NY, 2, ROWS, FEAT), BF),
            pltpu.VMEM((NB, NY - 1, 2, ROWS, FEAT), BF),
            pltpu.VMEM((NB, 2, 2, ROWS, FEAT), BF),
            pltpu.VMEM((NB, NX, 2, 2, CHUNK, FEAT), BF),
            pltpu.VMEM((NZ, 2, TOK, FEAT), F32),
            pltpu.VMEM((NZ, 2, TOK, FEAT), BF),
            pltpu.VMEM((NZ, 2, TOK, FEAT), BF),
            pltpu.VMEM((2, TOK, FEAT), F32),
            pltpu.VMEM((NZ, TOP, TOK), F32),
            pltpu.VMEM((NZ, TOP, TOK), F32),
            pltpu.VMEM((NZ, TOP, TOK), F32),
            pltpu.VMEM((TOP, TOK), F32),
            pltpu.VMEM((NT - 1, TOP, TOK), F32),
            pltpu.VMEM((NT, 8, FEAT), F32),
            pltpu.VMEM((NT, 8, FEAT), F32),
            pltpu.VMEM((NX, 8, FEAT), F32),
            pltpu.VMEM((NZ, 8, FEAT), F32),
            *dma(2 * (NT - 1), 32, NB * (NX - 1), NB * (NY - 1), NB),
            *dma(NB, NB * (NY - 1), NB * (NX - 1), 32, 2 * (NT - 1)),
            *dma(16, NT - 1, NT - 1, NX - 1, 16, NT - 1),
            pltpu.SemaphoreType.DMA((2 + 3 * NB,)),
        ],
        compiler_params=pltpu.CompilerParams(
            collective_id=0, has_side_effects=True, vmem_limit_bytes=60 * 2**20
        ),
        name="experts",
    )(normed, cotangent, meta, rmat, tri, gate_up, down_proj)


def shards(tokens, cotangent, gain, expert_ids, gate_probs, gate_up_weight, down_weight):
    t = lax.axis_index("tensor")
    values = tokens.astype(F32)
    inv_rms = lax.rsqrt(jnp.mean(values * values, axis=1, keepdims=True) + 1e-06)
    scaled = values * inv_rms
    normed = (scaled * gain[None, :]).astype(BF)
    probs_t = gate_probs.T
    high = lax.reduce_precision(probs_t, 8, 7)
    low = probs_t - high
    meta = jnp.concatenate(
        [
            jnp.concatenate([expert_ids.T.astype(F32), high], axis=0),
            jnp.concatenate([low, jnp.zeros_like(low)], axis=0),
        ],
        axis=1,
    ).astype(BF)
    summed, prob_sums, gain_sums, gate_up_grad, down_grad = experts(
        normed, cotangent, meta, gate_up_weight[0], down_weight[0]
    )
    mixed = (values + summed[0]).astype(BF)
    gain_side = summed[1] * gain[None, :]
    token_grad = (
        cotangent.astype(F32)
        + inv_rms * (gain_side - scaled * jnp.mean(gain_side * scaled, axis=1, keepdims=True))
    ).astype(BF)
    prob_grad = lax.dynamic_slice_in_dim(prob_sums, t * OWN, OWN, axis=1).T
    gain_grad = gain_sums[:, 0].reshape(-1) / gain
    return (mixed, token_grad, prob_grad, gain_grad, gate_up_grad[None], down_grad[None])


def solution(mesh):
    both = P(("expert", "tensor"), None)
    cube = P(("expert", "tensor"), None, None)
    in_specs = (both, both, P(), P("expert", None), P("expert", None), cube, cube)
    out_specs = (both, both, both, P(), cube, cube)
    return jax.shard_map(shards, mesh=mesh, in_specs=in_specs, out_specs=out_specs, check_vma=False)
```

```python
import jax
import jax.numpy as jnp
import numpy as np
from jax import lax
from jax.experimental import pallas as pl
from jax.experimental.pallas import tpu as pltpu
from jax.sharding import PartitionSpec as P

TOP = 8
NZ, NX, NY, NC = 16, 4, 4, 2
NT = NY * NC
TOK = 128
OWN = 16
CAP = 12
FEAT = 256
BATCH = 4
NB = NZ // BATCH
CHUNK = BATCH * CAP
ROWS = NX * CHUNK
SLOTS = NX * 2 * CHUNK
WIDE = BATCH * TOK
ORDER = [0, 1, -1, 2, -2, 3, -3, 4, -4, 5, -5, 6, -6, 7, -7, 8]
SLOT_OF = {d: s for s, d in enumerate(ORDER)}
SLOT_OF[-8] = SLOT_OF[8]
BF, F32 = jnp.bfloat16, jnp.float32
ACROSS = (((1,), (1,)), ((), ()))
OVER = (((0,), (0,)), ((), ()))


def place():
    e, t = lax.axis_index("expert"), lax.axis_index("tensor")
    return e, t, e // NX, lax.rem(e, NX), t // NC, lax.rem(t, NC)


def remote(src, dst, send, recv, device):
    return pltpu.make_async_remote_copy(
        src_ref=src, dst_ref=dst, send_sem=send, recv_sem=recv,
        device_id=device, device_id_type=pl.DeviceIdType.MESH,
    )


def greet(e, t, z, x):
    barrier = pltpu.get_barrier_semaphore()
    peers = [(e, lax.rem(t + i, NT)) for i in range(1, NT)]
    peers += [(z * NX + lax.rem(x + i, NX), t) for i in range(1, NX)]
    peers += [(lax.rem(z + i, NZ) * NX + x, t) for i in (1, NZ - 1)]
    for peer in peers:
        pl.semaphore_signal(barrier, inc=1, device_id=peer, device_id_type=pl.DeviceIdType.MESH)
    pl.semaphore_wait(barrier, len(peers))


def experts_kernel(
    normed_ref, cot_ref, meta_ref, rmat_ref, tri_ref, up_ref, down_ref,
    out_ref, prob_ref, gain_ref, up_grad_ref, down_grad_ref,
    zbuf, xs, yb, select, routed, parts, hid, joined,
    cb, ys, yr, q, xb, dense, ring_out, ring_in, total,
    pdense, pring_out, pring_in, ptotal, pgot, gsend, gone, gx, gz,
    a_send, a_recv, z_send, z_recv, x_send, x_recv, y_send, y_recv, c_send, c_recv,
    c2_send, c2_recv, y2_send, y2_recv, x2_send, x2_recv, z2_send, z2_recv, a2_send, a2_recv,
    p_send, p_recv, pa_send, pa_recv, g1_send, g1_recv, g2_send, g2_recv, g3_send, g3_recv,
    g4_send, g4_recv, local,
):
    e, t, z, x, y, c = place()
    phi = c * NY + y
    half = y // 2
    width = hid.shape[1]
    greet(e, t, z, x)
    started = []

    def feat(index):
        return pl.ds(pl.multiple_of(index * FEAT, FEAT), FEAT)

    def core_half(index):
        return pl.ds(pl.multiple_of(index * (NY * FEAT), NY * FEAT), NY * FEAT)

    def block16(index, size):
        return pl.ds(pl.multiple_of(index * size, 16), size)

    def go(src, dst, send, recv, n, device):
        copy = remote(src, dst, send.at[n], recv.at[n], device)
        copy.start()
        started.append(copy)
        return copy

    def others():
        return [(i, lax.rem(t + i, NT)) for i in range(1, NT)]

    def phi_of(other):
        return lax.rem(other, NC) * NY + other // NC

    right = (lax.rem(z + 1, NZ) * NX + x, t)
    left = (lax.rem(z + NZ - 1, NZ) * NX + x, t)

    stays = []
    arrivals = []
    for arr, ref in enumerate((normed_ref, cot_ref)):
        row_at = block16(arr * (TOK // OWN) + t, OWN)
        for i, other in others():
            n = arr * (NT - 1) + i - 1
            arrivals.append(
                go(ref.at[:, feat(phi_of(other))], zbuf.at[0, row_at, :], a_send, a_recv, n, (e, other))
            )
        stay = pltpu.make_async_copy(ref.at[:, feat(phi)], zbuf.at[0, row_at, :], local.at[arr])
        stay.start()
        stays.append(stay)
    zbuf[0, 2 * TOK :, :] = meta_ref[...]
    for copy in arrivals:
        copy.wait_recv()
    for stay in stays:
        stay.wait()

    pieces = (pl.ds(0, 96), pl.ds(96, 96), pl.ds(192, 80))

    def hop(step, way, p):
        sign = -1 if way == 0 else 1
        src, dst = SLOT_OF[sign * (step - 1)], SLOT_OF[sign * step]
        return go(
            zbuf.at[src, pieces[p], :], zbuf.at[dst, pieces[p], :], z_send, z_recv,
            (way * 8 + step - 1) * len(pieces) + p, right if way == 0 else left,
        )

    def named_experts():
        base = lax.convert_element_type(z * (2 * NX), F32)
        return base + lax.broadcasted_iota(jnp.int32, (8, TOK), 0).astype(F32)

    def stage_x(b):
        named = named_experts()
        chosen, high, low = [], [], []
        for j in range(BATCH):
            meta = zbuf[b * BATCH + j, 2 * TOK :, :].astype(F32)
            got, hi, lo = jnp.zeros((8, TOK), F32), jnp.zeros((8, TOK), F32), jnp.zeros((8, TOK), F32)
            for k in range(TOP):
                same = meta[k : k + 1, :TOK] == named
                got = got + jnp.where(same, 1.0, 0.0)
                hi = hi + jnp.where(same, meta[8 + k : 9 + k, :TOK], 0.0)
                lo = lo + jnp.where(same, meta[k : k + 1, TOK:], 0.0)
            chosen.append(got)
            high.append(hi)
            low.append(lo)
        taken = jnp.concatenate(chosen, axis=0)
        rank = jnp.dot(taken.astype(BF), tri_ref[...], preferred_element_type=F32)
        code = jnp.where(taken > 0.5, rank, -1.0)
        codes = jnp.concatenate(
            [
                jnp.concatenate([code[8 * j : 8 * j + 8] for j in range(BATCH)], axis=1),
                jnp.concatenate(high, axis=1),
                jnp.concatenate(low, axis=1),
            ],
            axis=0,
        )
        for f in range(2 * NX):
            hit = codes[f : f + 1, :] == rmat_ref[...]
            rows = pl.ds(f * CHUNK, CHUNK)
            select[b, 0, rows, :] = jnp.where(hit, 1.0, 0.0).astype(BF)
            select[b, 1, rows, :] = jnp.where(hit, codes[8 + f : 9 + f, :], 0.0).astype(BF)
            select[b, 2, rows, :] = jnp.where(hit, codes[16 + f : 17 + f, :], 0.0).astype(BF)
        these = pl.ds(b * BATCH, BATCH)
        normed = zbuf[these, 0:TOK, :].reshape(WIDE, FEAT)
        cot = zbuf[these, TOK : 2 * TOK, :].reshape(WIDE, FEAT)
        picked = jnp.dot(select[b, 0], normed, preferred_element_type=F32).astype(BF)
        grads = (
            jnp.dot(select[b, 1], cot, preferred_element_type=F32)
            + jnp.dot(select[b, 2], cot, preferred_element_type=F32)
        ).astype(BF)
        xs[b, :, :, 0] = picked.reshape(NX, 2, CHUNK, FEAT)
        xs[b, :, :, 1] = grads.reshape(NX, 2, CHUNK, FEAT)
        at = block16(x, CHUNK)
        copies = []
        for i in range(1, NX):
            other = lax.rem(x + i, NX)
            copies.append(
                go(
                    xs.at[b, other], yb.at[b, :, :, at, :], x_send, x_recv,
                    b * (NX - 1) + i - 1, (z * NX + other, t),
                )
            )
        stay = pltpu.make_async_copy(xs.at[b, x], yb.at[b, :, :, at, :], local.at[2 + b])
        stay.start()
        return copies, stay

    def stage_y(b, earlier):
        copies, stay = earlier
        for copy in copies:
            copy.wait_recv()
        stay.wait()
        where = pl.ds(b * ROWS, ROWS)
        sent = []
        for i in range(1, NY):
            other = lax.rem(y + i, NY)
            sent.append(
                go(
                    yb.at[b, other // 2], routed.at[:, where, feat(phi)], y_send, y_recv,
                    b * (NY - 1) + i - 1, (e, other * NC + c),
                )
            )
        keep = pltpu.make_async_copy(yb.at[b, half], routed.at[:, where, feat(phi)], local.at[2 + NB + b])
        keep.start()
        return sent, keep

    def stage_c(b, earlier):
        sent, keep = earlier
        for copy in sent:
            copy.wait_recv()
        keep.wait()
        block = routed.at[:, pl.ds(b * ROWS, ROWS), core_half(c)]
        return go(block, block, c_send, c_recv, b, (e, y * NC + 1 - c))

    def compute(b, earlier):
        earlier.wait_recv()
        where = pl.ds(b * ROWS, ROWS)
        projected = jnp.dot(routed[0, where, :], up_ref[...], preferred_element_type=F32)
        gate_pre, up_pre = projected[:, :width], projected[:, width:]
        sig = jax.nn.sigmoid(gate_pre)
        hidden = (gate_pre * sig * up_pre).astype(BF)
        hid[where, :] = hidden
        hidden_grad = lax.dot_general(routed[1, where, :], down_ref[...], ACROSS, preferred_element_type=F32)
        both = jnp.concatenate(
            [
                hidden_grad * up_pre * sig * (1.0 + gate_pre * (1.0 - sig)),
                hidden_grad * gate_pre * sig,
            ],
            axis=1,
        ).astype(BF)
        joined[where, :] = both
        for n in range(4):
            cols = pl.ds(n * 2 * FEAT, 2 * FEAT)
            parts[0, where, cols] = jnp.dot(hidden, down_ref[:, cols], preferred_element_type=F32).astype(BF)
            parts[1, where, cols] = lax.dot_general(
                both, up_ref[cols, :], ACROSS, preferred_element_type=F32
            ).astype(BF)
        return go(parts.at[:, where, core_half(1 - c)], cb.at[b], c2_send, c2_recv, b, (e, y * NC + 1 - c))

    def weight_grads():
        for n in range(4):
            cols = pl.ds(n * 2 * FEAT, 2 * FEAT)
            down_grad_ref[:, cols] = lax.dot_general(
                hid[...], routed[1, :, cols], OVER, preferred_element_type=F32
            ).astype(BF)
            grad = lax.dot_general(routed[0, :, cols], joined[...], OVER, preferred_element_type=F32)
            up_grad_ref[cols, :] = grad.astype(BF)
            summed = lax.dot_general(
                jnp.ones((8, 2 * width), F32), grad * up_ref[cols, :].astype(F32), ACROSS,
                precision=lax.Precision.HIGHEST, preferred_element_type=F32,
            )
            gsend[2 * n] = summed[:, :FEAT]
            gsend[2 * n + 1] = summed[:, FEAT:]

    def back_y(b, earlier):
        earlier.wait_recv()
        for k in range(NY):
            mine = parts[:, pl.ds(b * ROWS, ROWS), feat(c * NY + k)]
            theirs = cb[b, :, :, k * FEAT : (k + 1) * FEAT]
            ys[b, k] = (mine.astype(F32) + theirs.astype(F32)).astype(BF)
        sent = []
        for i in range(1, NY):
            other = lax.rem(y + i, NY)
            sent.append(
                go(
                    ys.at[b, other], yr.at[b, i - 1], y2_send, y2_recv,
                    b * (NY - 1) + i - 1, (e, other * NC + c),
                )
            )
        return sent

    def back_x(b, sent):
        for copy in sent:
            copy.wait_recv()
        odd = lax.rem(y, 2)
        partner = 2 * (1 - odd)
        q[b, half] = (ys[b, y].astype(F32) + yr[b, partner].astype(F32)).astype(BF)
        q[b, 1 - half] = (yr[b, 1].astype(F32) + yr[b, 2 * odd].astype(F32)).astype(BF)
        copies = []
        for i in range(1, NX):
            other = lax.rem(x + i, NX)
            copies.append(
                go(
                    q.at[b, :, :, block16(other, CHUNK), :], xb.at[b, x], x2_send, x2_recv,
                    b * (NX - 1) + i - 1, (z * NX + other, t),
                )
            )
        stay = pltpu.make_async_copy(
            q.at[b, :, :, block16(x, CHUNK), :], xb.at[b, x], local.at[2 + 2 * NB + b]
        )
        stay.start()
        return copies, stay

    def spread(b, earlier):
        copies, stay = earlier
        these = pl.ds(b * BATCH, BATCH)
        cot = zbuf[these, TOK : 2 * TOK, :].reshape(WIDE, FEAT)
        cot_slots = jnp.dot(select[b, 0], cot, preferred_element_type=F32)
        for copy in copies:
            copy.wait_recv()
        stay.wait()
        outs = xb[b, :, :, 0].reshape(SLOTS, FEAT)
        grads = xb[b, :, :, 1].reshape(SLOTS, FEAT)
        first = lax.dot_general(select[b, 1], outs, OVER, preferred_element_type=F32)
        first = first + lax.dot_general(select[b, 2], outs, OVER, preferred_element_type=F32)
        second = lax.dot_general(select[b, 0], grads, OVER, preferred_element_type=F32)
        for j in range(BATCH):
            dense[b * BATCH + j, 0] = first[j * TOK : (j + 1) * TOK]
            dense[b * BATCH + j, 1] = second[j * TOK : (j + 1) * TOK]
        value = jnp.sum(cot_slots * outs.astype(F32), axis=1, keepdims=True)
        by_expert = jnp.concatenate(
            [
                jnp.sum(
                    select[b, 0, f * CHUNK : (f + 1) * CHUNK, :].astype(F32)
                    * value[f * CHUNK : (f + 1) * CHUNK],
                    axis=0, keepdims=True,
                )
                for f in range(2 * NX)
            ],
            axis=0,
        )
        named = named_experts()
        for j in range(BATCH):
            ids = zbuf[b * BATCH + j, 2 * TOK :, :TOK].astype(F32)
            mine = by_expert[:, j * TOK : (j + 1) * TOK]
            pdense[b * BATCH + j] = jnp.concatenate(
                [
                    jnp.sum(jnp.where(ids[k : k + 1] == named, mine, 0.0), axis=0, keepdims=True)
                    for k in range(TOP)
                ],
                axis=0,
            )

    ring = {}

    def back_hop(step):
        ways = (0, 1) if step < 7 else (0,)
        device = (right, left)
        slot = (SLOT_OF[8 - step], SLOT_OF[-(7 - step)])
        for arr in range(2):
            for part in range(2):
                some = pl.ds(part * (TOK // 2), TOK // 2)
                for way in ways:
                    n = way * 8 + step
                    value = dense[slot[way], arr, some, :]
                    if step > 0:
                        ring[way, step - 1, arr, part].wait_recv()
                        value = value + ring_in[n - 1, arr, some, :].astype(F32)
                    ring_out[n, arr, some, :] = value.astype(BF)
                    ring[way, step, arr, part] = go(
                        ring_out.at[n, arr, some, :], ring_in.at[n, arr, some, :], z2_send, z2_recv,
                        4 * n + 2 * arr + part, device[way],
                    )
        for way in ways:
            n = way * 8 + step
            value = pdense[slot[way]]
            if step > 0:
                ring[way, step - 1, "prob"].wait_recv()
                ring[way, step - 1, "gain"].wait_recv()
                value = value + pring_in[n - 1]
            pring_out[n] = value
            ring[way, step, "prob"] = go(pring_out.at[n], pring_in.at[n], p_send, p_recv, n, device[way])
            origin = lax.rem(z - step + NZ, NZ) if way == 0 else lax.rem(z + step, NZ)
            ring[way, step, "gain"] = go(gz.at[origin], gz.at[origin], g3_send, g3_recv, n, device[way])

    flying = {}
    for p in range(len(pieces)):
        for way in range(2):
            flying[way, p] = hop(1, way, p)
    xdone, ydone, cdone, back = {}, {}, {}, {}
    for step in range(1, 9):
        for p in range(len(pieces)):
            for way in range(2):
                last = 8 if way == 0 else 7
                if step > last:
                    continue
                flying[way, p].wait_recv()
                if step < last:
                    flying[way, p] = hop(step + 1, way, p)
        b = step // 2 - 1
        if step % 2 == 0:
            xdone[b] = stage_x(b)
            if b >= 2:
                cdone[b - 2] = stage_c(b - 2, ydone[b - 2])
        elif b >= 0:
            ydone[b] = stage_y(b, xdone[b])
    ydone[3] = stage_y(3, xdone[3])
    back[0] = compute(0, cdone[0])
    cdone[2] = stage_c(2, ydone[2])
    back[1] = compute(1, cdone[1])
    back[2] = compute(2, cdone[2])
    cdone[3] = stage_c(3, ydone[3])
    back[3] = compute(3, cdone[3])

    ysent, xsent = {3: back_y(3, back[3])}, {}
    weight_grads()
    ysent[2] = back_y(2, back[2])
    gains = []
    for i, other in others():
        their = phi_of(other)
        gains.append(go(gsend.at[their], gone.at[i], g1_send, g1_recv, i - 1, (e, other)))
    gone[0] = gsend[phi]
    xsent[3] = back_x(3, ysent[3])
    ysent[1] = back_y(1, back[1])
    for copy in gains:
        copy.wait_recv()
    gain_sum = gone[0]
    for i in range(1, NT):
        gain_sum = gain_sum + gone[i]
    gx[x] = gain_sum
    gains = []
    for i in range(1, NX):
        other = lax.rem(x + i, NX)
        gains.append(go(gx.at[x], gx.at[x], g2_send, g2_recv, i - 1, (z * NX + other, t)))
    spread(3, xsent[3])
    for copy in gains:
        copy.wait_recv()
    gz[z] = gx[0] + gx[1] + gx[2] + gx[3]
    back_hop(0)
    xsent[2] = back_x(2, ysent[2])
    ysent[0] = back_y(0, back[0])
    back_hop(1)
    spread(2, xsent[2])
    back_hop(2)
    xsent[1] = back_x(1, ysent[1])
    back_hop(3)
    spread(1, xsent[1])
    back_hop(4)
    xsent[0] = back_x(0, ysent[0])
    back_hop(5)
    spread(0, xsent[0])
    back_hop(6)
    back_hop(7)

    finals = []
    for arr in range(2):
        for part in range(2):
            ring[0, 7, arr, part].wait_recv()
            ring[1, 6, arr, part].wait_recv()
        total[arr] = dense[0, arr] + ring_in[7, arr].astype(F32) + ring_in[8 + 6, arr].astype(F32)
        for i, other in others():
            n = arr * (NT - 1) + i - 1
            finals.append(
                go(
                    total.at[arr, block16(other, OWN), :], out_ref.at[arr, :, feat(phi)],
                    a2_send, a2_recv, n, (e, other),
                )
            )
        stay = pltpu.make_async_copy(
            total.at[arr, block16(t, OWN), :], out_ref.at[arr, :, feat(phi)], local.at[arr]
        )
        stay.start()
        stays.append(stay)
    for way in range(2):
        for kind in ("prob", "gain"):
            ring[way, 7 - way, kind].wait_recv()
    ptotal[...] = pdense[0] + pring_in[7] + pring_in[8 + 6]
    gain_sum = gz[0]
    for n in range(1, NZ):
        gain_sum = gain_sum + gz[n]
    gain_ref[phi] = gain_sum
    for i, other in others():
        finals.append(go(ptotal, pgot.at[i - 1], pa_send, pa_recv, i - 1, (e, other)))
        finals.append(go(gain_ref.at[phi], gain_ref.at[phi], g4_send, g4_recv, i - 1, (e, other)))
    for copy in finals:
        copy.wait_recv()
    for stay in stays[2:]:
        stay.wait()
    prob_sum = ptotal[...]
    for i in range(NT - 1):
        prob_sum = prob_sum + pgot[i]
    prob_ref[...] = prob_sum
    for copy in started:
        copy.wait_send()


def vmem():
    return pl.BlockSpec(memory_space=pltpu.VMEM)


def dma(*counts):
    return [pltpu.SemaphoreType.DMA((n,)) for n in counts for _ in range(2)]


def constants():
    lane = np.arange(WIDE)
    row = np.arange(CHUNK)
    rmat = np.where(lane[None, :] // TOK == row[:, None] // CAP, row[:, None] % CAP, -5)
    tri = np.arange(TOK)[:, None] < np.arange(TOK)[None, :]
    return jnp.asarray(rmat, F32), jnp.asarray(tri, BF)


def experts(normed, cotangent, meta, gate_up, down_proj):
    features, hidden = NT * FEAT, down_proj.shape[0]
    rows = NB * ROWS
    shape = jax.ShapeDtypeStruct
    rmat, tri = constants()
    return pl.pallas_call(
        experts_kernel,
        out_shape=(
            shape((2, OWN, features), F32),
            shape((TOP, TOK), F32),
            shape((NT, 8, FEAT), F32),
            shape((features, 2 * hidden), BF),
            shape((hidden, features), BF),
        ),
        in_specs=[vmem()] * 7,
        out_specs=tuple([vmem()] * 5),
        scratch_shapes=[
            pltpu.VMEM((NZ, 2 * TOK + OWN, FEAT), BF),
            pltpu.VMEM((NB, NX, 2, 2, CHUNK, FEAT), BF),
            pltpu.VMEM((NB, 2, 2, ROWS, FEAT), BF),
            pltpu.VMEM((NB, 3, SLOTS, WIDE), BF),
            pltpu.VMEM((2, rows, features), BF),
            pltpu.VMEM((2, rows, features), BF),
            pltpu.VMEM((rows, hidden), BF),
            pltpu.VMEM((rows, 2 * hidden), BF),
            pltpu.VMEM((NB, 2, ROWS, NY * FEAT), BF),
            pltpu.VMEM((NB, NY, 2, ROWS, FEAT), BF),
            pltpu.VMEM((NB, NY - 1, 2, ROWS, FEAT), BF),
            pltpu.VMEM((NB, 2, 2, ROWS, FEAT), BF),
            pltpu.VMEM((NB, NX, 2, 2, CHUNK, FEAT), BF),
            pltpu.VMEM((NZ, 2, TOK, FEAT), F32),
            pltpu.VMEM((NZ, 2, TOK, FEAT), BF),
            pltpu.VMEM((NZ, 2, TOK, FEAT), BF),
            pltpu.VMEM((2, TOK, FEAT), F32),
            pltpu.VMEM((NZ, TOP, TOK), F32),
            pltpu.VMEM((NZ, TOP, TOK), F32),
            pltpu.VMEM((NZ, TOP, TOK), F32),
            pltpu.VMEM((TOP, TOK), F32),
            pltpu.VMEM((NT - 1, TOP, TOK), F32),
            pltpu.VMEM((NT, 8, FEAT), F32),
            pltpu.VMEM((NT, 8, FEAT), F32),
            pltpu.VMEM((NX, 8, FEAT), F32),
            pltpu.VMEM((NZ, 8, FEAT), F32),
            *dma(2 * (NT - 1), 48, NB * (NX - 1), NB * (NY - 1), NB),
            *dma(NB, NB * (NY - 1), NB * (NX - 1), 64, 2 * (NT - 1)),
            *dma(16, NT - 1, NT - 1, NX - 1, 16, NT - 1),
            pltpu.SemaphoreType.DMA((2 + 3 * NB,)),
        ],
        compiler_params=pltpu.CompilerParams(
            collective_id=0, has_side_effects=True, vmem_limit_bytes=60 * 2**20
        ),
        name="experts",
    )(normed, cotangent, meta, rmat, tri, gate_up, down_proj)


def shards(tokens, cotangent, gain, expert_ids, gate_probs, gate_up_weight, down_weight):
    t = lax.axis_index("tensor")
    values = tokens.astype(F32)
    inv_rms = lax.rsqrt(jnp.mean(values * values, axis=1, keepdims=True) + 1e-06)
    scaled = values * inv_rms
    normed = (scaled * gain[None, :]).astype(BF)
    probs_t = gate_probs.T
    high = lax.reduce_precision(probs_t, 8, 7)
    low = probs_t - high
    meta = jnp.concatenate(
        [
            jnp.concatenate([expert_ids.T.astype(F32), high], axis=0),
            jnp.concatenate([low, jnp.zeros_like(low)], axis=0),
        ],
        axis=1,
    ).astype(BF)
    summed, prob_sums, gain_sums, gate_up_grad, down_grad = experts(
        normed, cotangent, meta, gate_up_weight[0], down_weight[0]
    )
    mixed = (values + summed[0]).astype(BF)
    gain_side = summed[1] * gain[None, :]
    token_grad = (
        cotangent.astype(F32)
        + inv_rms * (gain_side - scaled * jnp.mean(gain_side * scaled, axis=1, keepdims=True))
    ).astype(BF)
    prob_grad = lax.dynamic_slice_in_dim(prob_sums, t * OWN, OWN, axis=1).T
    gain_grad = gain_sums[:, 0].reshape(-1) / gain
    return (mixed, token_grad, prob_grad, gain_grad, gate_up_grad[None], down_grad[None])


def solution(mesh):
    both = P(("expert", "tensor"), None)
    cube = P(("expert", "tensor"), None, None)
    in_specs = (both, both, P(), P("expert", None), P("expert", None), cube, cube)
    out_specs = (both, both, both, P(), cube, cube)
    return jax.shard_map(shards, mesh=mesh, in_specs=in_specs, out_specs=out_specs, check_vma=False)
```

```python
import jax
import jax.numpy as jnp
import numpy as np
from jax import lax
from jax.experimental import pallas as pl
from jax.experimental.pallas import tpu as pltpu
from jax.sharding import PartitionSpec as P

TOP = 8
NZ, NX, NY, NC = 16, 4, 4, 2
NT = NY * NC
TOK = 128
OWN = 16
CAP = 12
FEAT = 256
BATCH = 4
NB = NZ // BATCH
CHUNK = BATCH * CAP
ROWS = NX * CHUNK
SLOTS = NX * 2 * CHUNK
WIDE = BATCH * TOK
ORDER = [0, 1, -1, 2, -2, 3, -3, 4, -4, 5, -5, 6, -6, 7, -7, 8]
SLOT_OF = {d: s for s, d in enumerate(ORDER)}
SLOT_OF[-8] = SLOT_OF[8]
BF, F32 = jnp.bfloat16, jnp.float32
ACROSS = (((1,), (1,)), ((), ()))
OVER = (((0,), (0,)), ((), ()))


def place():
    e, t = lax.axis_index("expert"), lax.axis_index("tensor")
    return e, t, e // NX, lax.rem(e, NX), t // NC, lax.rem(t, NC)


def remote(src, dst, send, recv, device):
    return pltpu.make_async_remote_copy(
        src_ref=src, dst_ref=dst, send_sem=send, recv_sem=recv,
        device_id=device, device_id_type=pl.DeviceIdType.MESH,
    )


def greet(e, t, z, x):
    barrier = pltpu.get_barrier_semaphore()
    peers = [(e, lax.rem(t + i, NT)) for i in range(1, NT)]
    peers += [(z * NX + lax.rem(x + i, NX), t) for i in range(1, NX)]
    peers += [(lax.rem(z + i, NZ) * NX + x, t) for i in (1, NZ - 1)]
    for peer in peers:
        pl.semaphore_signal(barrier, inc=1, device_id=peer, device_id_type=pl.DeviceIdType.MESH)
    return barrier, len(peers)


def experts_kernel(
    token_ref, cot_ref, weight_ref, ids_ref, probs_ref, rmat_ref, tri_ref, up_ref, down_ref,
    mixed_ref, token_grad_ref, prob_ref, gain_out_ref, up_grad_ref, down_grad_ref,
    normed_ref, out_ref, gain_ref, prob_tall,
    zbuf, xs, yb, select, routed, parts, hid, joined,
    cb, ys, yr, q, xb, dense, ring_out, ring_in, total,
    pdense, pring_out, pring_in, ptotal, pgot, gsend, gone, gx, gz,
    a_send, a_recv, z_send, z_recv, x_send, x_recv, y_send, y_recv, c_send, c_recv,
    c2_send, c2_recv, y2_send, y2_recv, x2_send, x2_recv, z2_send, z2_recv, a2_send, a2_recv,
    p_send, p_recv, pa_send, pa_recv, g1_send, g1_recv, g2_send, g2_recv, g3_send, g3_recv,
    g4_send, g4_recv, local,
):
    e, t, z, x, y, c = place()
    phi = c * NY + y
    half = y // 2
    width = hid.shape[1]
    barrier, count = greet(e, t, z, x)
    started = []

    def normalize():
        values = token_ref[...].astype(F32)
        inv_rms = lax.rsqrt(jnp.mean(values * values, axis=1, keepdims=True) + 1e-06)
        return values, inv_rms, values * inv_rms

    normed_ref[...] = (normalize()[2] * weight_ref[...]).astype(BF)
    probs = jnp.transpose(probs_ref[...])
    high = probs.astype(BF).astype(F32)
    low = probs - high
    ids = jnp.transpose(ids_ref[...].astype(F32))
    zbuf[0, 2 * TOK :, :TOK] = jnp.concatenate([ids, high], axis=0).astype(BF)
    zbuf[0, 2 * TOK :, TOK:] = jnp.concatenate([low, jnp.zeros_like(low)], axis=0).astype(BF)
    pl.semaphore_wait(barrier, count)

    def feat(index):
        return pl.ds(pl.multiple_of(index * FEAT, FEAT), FEAT)

    def core_half(index):
        return pl.ds(pl.multiple_of(index * (NY * FEAT), NY * FEAT), NY * FEAT)

    def block16(index, size):
        return pl.ds(pl.multiple_of(index * size, 16), size)

    def go(src, dst, send, recv, n, device):
        copy = remote(src, dst, send.at[n], recv.at[n], device)
        copy.start()
        started.append(copy)
        return copy

    def others():
        return [(i, lax.rem(t + i, NT)) for i in range(1, NT)]

    def phi_of(other):
        return lax.rem(other, NC) * NY + other // NC

    right = (lax.rem(z + 1, NZ) * NX + x, t)
    left = (lax.rem(z + NZ - 1, NZ) * NX + x, t)

    stays = []
    arrivals = []
    for arr, ref in enumerate((normed_ref, cot_ref)):
        row_at = block16(arr * (TOK // OWN) + t, OWN)
        for i, other in others():
            n = arr * (NT - 1) + i - 1
            arrivals.append(
                go(ref.at[:, feat(phi_of(other))], zbuf.at[0, row_at, :], a_send, a_recv, n, (e, other))
            )
        stay = pltpu.make_async_copy(ref.at[:, feat(phi)], zbuf.at[0, row_at, :], local.at[arr])
        stay.start()
        stays.append(stay)
    for copy in arrivals:
        copy.wait_recv()
    for stay in stays:
        stay.wait()

    pieces = (pl.ds(0, 96), pl.ds(96, 96), pl.ds(192, 80))

    def hop(step, way, p):
        sign = -1 if way == 0 else 1
        src, dst = SLOT_OF[sign * (step - 1)], SLOT_OF[sign * step]
        return go(
            zbuf.at[src, pieces[p], :], zbuf.at[dst, pieces[p], :], z_send, z_recv,
            (way * 8 + step - 1) * len(pieces) + p, right if way == 0 else left,
        )

    def named_experts():
        base = lax.convert_element_type(z * (2 * NX), F32)
        return base + lax.broadcasted_iota(jnp.int32, (8, TOK), 0).astype(F32)

    def stage_x(b):
        named = named_experts()
        chosen, high, low = [], [], []
        for j in range(BATCH):
            meta = zbuf[b * BATCH + j, 2 * TOK :, :].astype(F32)
            got, hi, lo = jnp.zeros((8, TOK), F32), jnp.zeros((8, TOK), F32), jnp.zeros((8, TOK), F32)
            for k in range(TOP):
                same = meta[k : k + 1, :TOK] == named
                got = got + jnp.where(same, 1.0, 0.0)
                hi = hi + jnp.where(same, meta[8 + k : 9 + k, :TOK], 0.0)
                lo = lo + jnp.where(same, meta[k : k + 1, TOK:], 0.0)
            chosen.append(got)
            high.append(hi)
            low.append(lo)
        taken = jnp.concatenate(chosen, axis=0)
        rank = jnp.dot(taken.astype(BF), tri_ref[...], preferred_element_type=F32)
        code = jnp.where(taken > 0.5, rank, -1.0)
        codes = jnp.concatenate(
            [
                jnp.concatenate([code[8 * j : 8 * j + 8] for j in range(BATCH)], axis=1),
                jnp.concatenate(high, axis=1),
                jnp.concatenate(low, axis=1),
            ],
            axis=0,
        )
        for f in range(2 * NX):
            hit = codes[f : f + 1, :] == rmat_ref[...]
            rows = pl.ds(f * CHUNK, CHUNK)
            select[b, 0, rows, :] = jnp.where(hit, 1.0, 0.0).astype(BF)
            select[b, 1, rows, :] = jnp.where(hit, codes[8 + f : 9 + f, :], 0.0).astype(BF)
            select[b, 2, rows, :] = jnp.where(hit, codes[16 + f : 17 + f, :], 0.0).astype(BF)
        these = pl.ds(b * BATCH, BATCH)
        normed = zbuf[these, 0:TOK, :].reshape(WIDE, FEAT)
        cot = zbuf[these, TOK : 2 * TOK, :].reshape(WIDE, FEAT)
        picked = jnp.dot(select[b, 0], normed, preferred_element_type=F32).astype(BF)
        grads = (
            jnp.dot(select[b, 1], cot, preferred_element_type=F32)
            + jnp.dot(select[b, 2], cot, preferred_element_type=F32)
        ).astype(BF)
        xs[b, :, :, 0] = picked.reshape(NX, 2, CHUNK, FEAT)
        xs[b, :, :, 1] = grads.reshape(NX, 2, CHUNK, FEAT)
        at = block16(x, CHUNK)
        copies = []
        for i in range(1, NX):
            other = lax.rem(x + i, NX)
            copies.append(
                go(
                    xs.at[b, other], yb.at[b, :, :, at, :], x_send, x_recv,
                    b * (NX - 1) + i - 1, (z * NX + other, t),
                )
            )
        stay = pltpu.make_async_copy(xs.at[b, x], yb.at[b, :, :, at, :], local.at[2 + b])
        stay.start()
        return copies, stay

    def stage_y(b, earlier):
        copies, stay = earlier
        for copy in copies:
            copy.wait_recv()
        stay.wait()
        where = pl.ds(b * ROWS, ROWS)
        sent = []
        for i in range(1, NY):
            other = lax.rem(y + i, NY)
            sent.append(
                go(
                    yb.at[b, other // 2], routed.at[:, where, feat(phi)], y_send, y_recv,
                    b * (NY - 1) + i - 1, (e, other * NC + c),
                )
            )
        keep = pltpu.make_async_copy(yb.at[b, half], routed.at[:, where, feat(phi)], local.at[2 + NB + b])
        keep.start()
        return sent, keep

    def stage_c(b, earlier):
        sent, keep = earlier
        for copy in sent:
            copy.wait_recv()
        keep.wait()
        block = routed.at[:, pl.ds(b * ROWS, ROWS), core_half(c)]
        return go(block, block, c_send, c_recv, b, (e, y * NC + 1 - c))

    def compute(b, earlier):
        earlier.wait_recv()
        where = pl.ds(b * ROWS, ROWS)
        projected = jnp.dot(routed[0, where, :], up_ref[...], preferred_element_type=F32)
        gate_pre, up_pre = projected[:, :width], projected[:, width:]
        sig = jax.nn.sigmoid(gate_pre)
        hidden = (gate_pre * sig * up_pre).astype(BF)
        hid[where, :] = hidden
        hidden_grad = lax.dot_general(routed[1, where, :], down_ref[...], ACROSS, preferred_element_type=F32)
        both = jnp.concatenate(
            [
                hidden_grad * up_pre * sig * (1.0 + gate_pre * (1.0 - sig)),
                hidden_grad * gate_pre * sig,
            ],
            axis=1,
        ).astype(BF)
        joined[where, :] = both
        for n in range(4):
            cols = pl.ds(n * 2 * FEAT, 2 * FEAT)
            parts[0, where, cols] = jnp.dot(hidden, down_ref[:, cols], preferred_element_type=F32).astype(BF)
            parts[1, where, cols] = lax.dot_general(
                both, up_ref[cols, :], ACROSS, preferred_element_type=F32
            ).astype(BF)
        return go(parts.at[:, where, core_half(1 - c)], cb.at[b], c2_send, c2_recv, b, (e, y * NC + 1 - c))

    def weight_grads():
        for n in range(4):
            cols = pl.ds(n * 2 * FEAT, 2 * FEAT)
            down_grad_ref[:, cols] = lax.dot_general(
                hid[...], routed[1, :, cols], OVER, preferred_element_type=F32
            ).astype(BF)
            grad = lax.dot_general(routed[0, :, cols], joined[...], OVER, preferred_element_type=F32)
            up_grad_ref[cols, :] = grad.astype(BF)
            summed = lax.dot_general(
                jnp.ones((8, 2 * width), F32), grad * up_ref[cols, :].astype(F32), ACROSS,
                precision=lax.Precision.HIGHEST, preferred_element_type=F32,
            ) / weight_ref[:, cols]
            gsend[2 * n] = summed[:, :FEAT]
            gsend[2 * n + 1] = summed[:, FEAT:]

    def back_y(b, earlier):
        earlier.wait_recv()
        for k in range(NY):
            mine = parts[:, pl.ds(b * ROWS, ROWS), feat(c * NY + k)]
            theirs = cb[b, :, :, k * FEAT : (k + 1) * FEAT]
            ys[b, k] = (mine.astype(F32) + theirs.astype(F32)).astype(BF)
        sent = []
        for i in range(1, NY):
            other = lax.rem(y + i, NY)
            sent.append(
                go(
                    ys.at[b, other], yr.at[b, i - 1], y2_send, y2_recv,
                    b * (NY - 1) + i - 1, (e, other * NC + c),
                )
            )
        return sent

    def back_x(b, sent):
        for copy in sent:
            copy.wait_recv()
        odd = lax.rem(y, 2)
        partner = 2 * (1 - odd)
        q[b, half] = (ys[b, y].astype(F32) + yr[b, partner].astype(F32)).astype(BF)
        q[b, 1 - half] = (yr[b, 1].astype(F32) + yr[b, 2 * odd].astype(F32)).astype(BF)
        copies = []
        for i in range(1, NX):
            other = lax.rem(x + i, NX)
            copies.append(
                go(
                    q.at[b, :, :, block16(other, CHUNK), :], xb.at[b, x], x2_send, x2_recv,
                    b * (NX - 1) + i - 1, (z * NX + other, t),
                )
            )
        stay = pltpu.make_async_copy(
            q.at[b, :, :, block16(x, CHUNK), :], xb.at[b, x], local.at[2 + 2 * NB + b]
        )
        stay.start()
        return copies, stay

    def spread(b, earlier):
        copies, stay = earlier
        these = pl.ds(b * BATCH, BATCH)
        cot = zbuf[these, TOK : 2 * TOK, :].reshape(WIDE, FEAT)
        cot_slots = jnp.dot(select[b, 0], cot, preferred_element_type=F32)
        for copy in copies:
            copy.wait_recv()
        stay.wait()
        outs = xb[b, :, :, 0].reshape(SLOTS, FEAT)
        grads = xb[b, :, :, 1].reshape(SLOTS, FEAT)
        first = lax.dot_general(select[b, 1], outs, OVER, preferred_element_type=F32)
        first = first + lax.dot_general(select[b, 2], outs, OVER, preferred_element_type=F32)
        second = lax.dot_general(select[b, 0], grads, OVER, preferred_element_type=F32)
        for j in range(BATCH):
            dense[b * BATCH + j, 0] = first[j * TOK : (j + 1) * TOK]
            dense[b * BATCH + j, 1] = second[j * TOK : (j + 1) * TOK]
        value = jnp.sum(cot_slots * outs.astype(F32), axis=1, keepdims=True)
        by_expert = jnp.concatenate(
            [
                jnp.sum(
                    select[b, 0, f * CHUNK : (f + 1) * CHUNK, :].astype(F32)
                    * value[f * CHUNK : (f + 1) * CHUNK],
                    axis=0, keepdims=True,
                )
                for f in range(2 * NX)
            ],
            axis=0,
        )
        named = named_experts()
        for j in range(BATCH):
            ids = zbuf[b * BATCH + j, 2 * TOK :, :TOK].astype(F32)
            mine = by_expert[:, j * TOK : (j + 1) * TOK]
            pdense[b * BATCH + j] = jnp.concatenate(
                [
                    jnp.sum(jnp.where(ids[k : k + 1] == named, mine, 0.0), axis=0, keepdims=True)
                    for k in range(TOP)
                ],
                axis=0,
            )

    ring = {}

    def back_hop(step):
        ways = (0, 1) if step < 7 else (0,)
        device = (right, left)
        slot = (SLOT_OF[8 - step], SLOT_OF[-(7 - step)])
        for arr in range(2):
            for part in range(2):
                some = pl.ds(part * (TOK // 2), TOK // 2)
                for way in ways:
                    n = way * 8 + step
                    value = dense[slot[way], arr, some, :]
                    if step > 0:
                        ring[way, step - 1, arr, part].wait_recv()
                        value = value + ring_in[n - 1, arr, some, :].astype(F32)
                    ring_out[n, arr, some, :] = value.astype(BF)
                    ring[way, step, arr, part] = go(
                        ring_out.at[n, arr, some, :], ring_in.at[n, arr, some, :], z2_send, z2_recv,
                        4 * n + 2 * arr + part, device[way],
                    )
        for way in ways:
            n = way * 8 + step
            value = pdense[slot[way]]
            if step > 0:
                ring[way, step - 1, "prob"].wait_recv()
                ring[way, step - 1, "gain"].wait_recv()
                value = value + pring_in[n - 1]
            pring_out[n] = value
            ring[way, step, "prob"] = go(pring_out.at[n], pring_in.at[n], p_send, p_recv, n, device[way])
            origin = lax.rem(z - step + NZ, NZ) if way == 0 else lax.rem(z + step, NZ)
            ring[way, step, "gain"] = go(gz.at[origin], gz.at[origin], g3_send, g3_recv, n, device[way])

    flying = {}
    for p in range(len(pieces)):
        for way in range(2):
            flying[way, p] = hop(1, way, p)
    xdone, ydone, cdone, back = {}, {}, {}, {}
    for step in range(1, 9):
        for p in range(len(pieces)):
            for way in range(2):
                last = 8 if way == 0 else 7
                if step > last:
                    continue
                flying[way, p].wait_recv()
                if step < last:
                    flying[way, p] = hop(step + 1, way, p)
        b = step // 2 - 1
        if step % 2 == 0:
            xdone[b] = stage_x(b)
            if b >= 2:
                cdone[b - 2] = stage_c(b - 2, ydone[b - 2])
        elif b >= 0:
            ydone[b] = stage_y(b, xdone[b])
    ydone[3] = stage_y(3, xdone[3])
    back[0] = compute(0, cdone[0])
    cdone[2] = stage_c(2, ydone[2])
    back[1] = compute(1, cdone[1])
    back[2] = compute(2, cdone[2])
    cdone[3] = stage_c(3, ydone[3])
    back[3] = compute(3, cdone[3])

    ysent, xsent = {3: back_y(3, back[3])}, {}
    weight_grads()
    ysent[2] = back_y(2, back[2])
    gains = []
    for i, other in others():
        their = phi_of(other)
        gains.append(go(gsend.at[their], gone.at[i], g1_send, g1_recv, i - 1, (e, other)))
    gone[0] = gsend[phi]
    xsent[3] = back_x(3, ysent[3])
    ysent[1] = back_y(1, back[1])
    for copy in gains:
        copy.wait_recv()
    gain_sum = gone[0]
    for i in range(1, NT):
        gain_sum = gain_sum + gone[i]
    gx[x] = gain_sum
    gains = []
    for i in range(1, NX):
        other = lax.rem(x + i, NX)
        gains.append(go(gx.at[x], gx.at[x], g2_send, g2_recv, i - 1, (z * NX + other, t)))
    spread(3, xsent[3])
    for copy in gains:
        copy.wait_recv()
    gz[z] = gx[0] + gx[1] + gx[2] + gx[3]
    back_hop(0)
    xsent[2] = back_x(2, ysent[2])
    ysent[0] = back_y(0, back[0])
    back_hop(1)
    spread(2, xsent[2])
    back_hop(2)
    xsent[1] = back_x(1, ysent[1])
    back_hop(3)
    spread(1, xsent[1])
    back_hop(4)
    xsent[0] = back_x(0, ysent[0])
    back_hop(5)
    spread(0, xsent[0])
    back_hop(6)
    back_hop(7)

    finals = []
    for arr in range(2):
        for part in range(2):
            ring[0, 7, arr, part].wait_recv()
            ring[1, 6, arr, part].wait_recv()
        total[arr] = dense[0, arr] + ring_in[7, arr].astype(F32) + ring_in[8 + 6, arr].astype(F32)
        for i, other in others():
            n = arr * (NT - 1) + i - 1
            finals.append(
                go(
                    total.at[arr, block16(other, OWN), :], out_ref.at[arr, :, feat(phi)],
                    a2_send, a2_recv, n, (e, other),
                )
            )
        stay = pltpu.make_async_copy(
            total.at[arr, block16(t, OWN), :], out_ref.at[arr, :, feat(phi)], local.at[arr]
        )
        stay.start()
        stays.append(stay)
    for way in range(2):
        for kind in ("prob", "gain"):
            ring[way, 7 - way, kind].wait_recv()
    ptotal[...] = pdense[0] + pring_in[7] + pring_in[8 + 6]
    gain_sum = gz[0]
    for n in range(1, NZ):
        gain_sum = gain_sum + gz[n]
    gain_ref[phi] = gain_sum
    for i, other in others():
        finals.append(go(ptotal, pgot.at[i - 1], pa_send, pa_recv, i - 1, (e, other)))
        finals.append(go(gain_ref.at[phi], gain_ref.at[phi], g4_send, g4_recv, i - 1, (e, other)))
    for copy in finals:
        copy.wait_recv()
    for stay in stays[2:]:
        stay.wait()
    prob_sum = ptotal[...]
    for i in range(NT - 1):
        prob_sum = prob_sum + pgot[i]
    prob_tall[...] = jnp.transpose(prob_sum)
    prob_ref[...] = prob_tall[block16(t, OWN), :]
    for n in range(NT):
        gain_out_ref[:, n * FEAT : (n + 1) * FEAT] = gain_ref[n, 0:1, :]
    values, inv_rms, scaled = normalize()
    mixed_ref[...] = (values + out_ref[0]).astype(BF)
    side = out_ref[1] * weight_ref[...]
    token_grad_ref[...] = (
        cot_ref[...].astype(F32)
        + inv_rms * (side - scaled * jnp.mean(side * scaled, axis=1, keepdims=True))
    ).astype(BF)
    for copy in started:
        copy.wait_send()


def vmem():
    return pl.BlockSpec(memory_space=pltpu.VMEM)


def dma(*counts):
    return [pltpu.SemaphoreType.DMA((n,)) for n in counts for _ in range(2)]


def constants():
    lane = np.arange(WIDE)
    row = np.arange(CHUNK)
    rmat = np.where(lane[None, :] // TOK == row[:, None] // CAP, row[:, None] % CAP, -5)
    tri = np.arange(TOK)[:, None] < np.arange(TOK)[None, :]
    return jnp.asarray(rmat, F32), jnp.asarray(tri, BF)


def experts(tokens, cotangent, gain, expert_ids, gate_probs, gate_up, down_proj):
    features, hidden = NT * FEAT, down_proj.shape[0]
    rows = NB * ROWS
    shape = jax.ShapeDtypeStruct
    rmat, tri = constants()
    return pl.pallas_call(
        experts_kernel,
        out_shape=(
            shape((OWN, features), BF),
            shape((OWN, features), BF),
            shape((OWN, TOP), F32),
            shape((1, features), F32),
            shape((features, 2 * hidden), BF),
            shape((hidden, features), BF),
        ),
        in_specs=[vmem()] * 9,
        out_specs=tuple([vmem()] * 6),
        scratch_shapes=[
            pltpu.VMEM((OWN, features), BF),
            pltpu.VMEM((2, OWN, features), F32),
            pltpu.VMEM((NT, 8, FEAT), F32),
            pltpu.VMEM((TOK, TOP), F32),
            pltpu.VMEM((NZ, 2 * TOK + OWN, FEAT), BF),
            pltpu.VMEM((NB, NX, 2, 2, CHUNK, FEAT), BF),
            pltpu.VMEM((NB, 2, 2, ROWS, FEAT), BF),
            pltpu.VMEM((NB, 3, SLOTS, WIDE), BF),
            pltpu.VMEM((2, rows, features), BF),
            pltpu.VMEM((2, rows, features), BF),
            pltpu.VMEM((rows, hidden), BF),
            pltpu.VMEM((rows, 2 * hidden), BF),
            pltpu.VMEM((NB, 2, ROWS, NY * FEAT), BF),
            pltpu.VMEM((NB, NY, 2, ROWS, FEAT), BF),
            pltpu.VMEM((NB, NY - 1, 2, ROWS, FEAT), BF),
            pltpu.VMEM((NB, 2, 2, ROWS, FEAT), BF),
            pltpu.VMEM((NB, NX, 2, 2, CHUNK, FEAT), BF),
            pltpu.VMEM((NZ, 2, TOK, FEAT), F32),
            pltpu.VMEM((NZ, 2, TOK, FEAT), BF),
            pltpu.VMEM((NZ, 2, TOK, FEAT), BF),
            pltpu.VMEM((2, TOK, FEAT), F32),
            pltpu.VMEM((NZ, TOP, TOK), F32),
            pltpu.VMEM((NZ, TOP, TOK), F32),
            pltpu.VMEM((NZ, TOP, TOK), F32),
            pltpu.VMEM((TOP, TOK), F32),
            pltpu.VMEM((NT - 1, TOP, TOK), F32),
            pltpu.VMEM((NT, 8, FEAT), F32),
            pltpu.VMEM((NT, 8, FEAT), F32),
            pltpu.VMEM((NX, 8, FEAT), F32),
            pltpu.VMEM((NZ, 8, FEAT), F32),
            *dma(2 * (NT - 1), 48, NB * (NX - 1), NB * (NY - 1), NB),
            *dma(NB, NB * (NY - 1), NB * (NX - 1), 64, 2 * (NT - 1)),
            *dma(16, NT - 1, NT - 1, NX - 1, 16, NT - 1),
            pltpu.SemaphoreType.DMA((2 + 3 * NB,)),
        ],
        compiler_params=pltpu.CompilerParams(
            collective_id=0, has_side_effects=True, vmem_limit_bytes=60 * 2**20
        ),
        name="experts",
    )(tokens, cotangent, gain, expert_ids, gate_probs, rmat, tri, gate_up, down_proj)


def shards(tokens, cotangent, gain, expert_ids, gate_probs, gate_up_weight, down_weight):
    mixed, token_grad, prob_grad, gain_grad, gate_up_grad, down_grad = experts(
        tokens, cotangent, gain[None], expert_ids, gate_probs, gate_up_weight[0], down_weight[0]
    )
    return (mixed, token_grad, prob_grad, gain_grad[0], gate_up_grad[None], down_grad[None])


def solution(mesh):
    both = P(("expert", "tensor"), None)
    cube = P(("expert", "tensor"), None, None)
    in_specs = (both, both, P(), P("expert", None), P("expert", None), cube, cube)
    out_specs = (both, both, both, P(), cube, cube)
    return jax.shard_map(shards, mesh=mesh, in_specs=in_specs, out_specs=out_specs, check_vma=False)
```

```python
import jax
import jax.numpy as jnp
import numpy as np
from jax import lax
from jax.experimental import pallas as pl
from jax.experimental.pallas import tpu as pltpu
from jax.sharding import PartitionSpec as P

TOP = 8
NZ, NX, NY, NC = 16, 4, 4, 2
NT = NY * NC
TOK = 128
OWN = 16
CAP = 12
FEAT = 256
BATCH = 4
NB = NZ // BATCH
CHUNK = BATCH * CAP
ROWS = NX * CHUNK
SLOTS = NX * 2 * CHUNK
WIDE = BATCH * TOK
ORDER = [0, 1, -1, 2, -2, 3, -3, 4, -4, 5, -5, 6, -6, 7, -7, 8]
SLOT_OF = {d: s for s, d in enumerate(ORDER)}
SLOT_OF[-8] = SLOT_OF[8]
BF, F32 = jnp.bfloat16, jnp.float32
ACROSS = (((1,), (1,)), ((), ()))
OVER = (((0,), (0,)), ((), ()))


def place():
    e, t = lax.axis_index("expert"), lax.axis_index("tensor")
    return e, t, e // NX, lax.rem(e, NX), t // NC, lax.rem(t, NC)


def remote(src, dst, send, recv, device):
    return pltpu.make_async_remote_copy(
        src_ref=src, dst_ref=dst, send_sem=send, recv_sem=recv,
        device_id=device, device_id_type=pl.DeviceIdType.MESH,
    )


def greet(e, t, z, x):
    barrier = pltpu.get_barrier_semaphore()
    peers = [(e, lax.rem(t + i, NT)) for i in range(1, NT)]
    peers += [(z * NX + lax.rem(x + i, NX), t) for i in range(1, NX)]
    peers += [(lax.rem(z + i, NZ) * NX + x, t) for i in (1, NZ - 1)]
    for peer in peers:
        pl.semaphore_signal(barrier, inc=1, device_id=peer, device_id_type=pl.DeviceIdType.MESH)
    return barrier, len(peers)


def experts_kernel(
    token_ref, cot_ref, weight_ref, ids_ref, probs_ref, rmat_ref, tri_ref, up_ref, down_ref,
    mixed_ref, token_grad_ref, prob_ref, gain_out_ref, up_grad_ref, down_grad_ref,
    normed_ref, out_ref, gain_ref, prob_tall,
    zbuf, xs, yb, select, routed, parts, hid, joined,
    cb, ys, yr, q, xb, dense, ring_out, ring_in, total,
    pdense, pring_out, pring_in, ptotal, pgot, gsend, gone, gx, gz,
    a_send, a_recv, z_send, z_recv, x_send, x_recv, y_send, y_recv, c_send, c_recv,
    c2_send, c2_recv, y2_send, y2_recv, x2_send, x2_recv, z2_send, z2_recv, a2_send, a2_recv,
    p_send, p_recv, pa_send, pa_recv, g1_send, g1_recv, g2_send, g2_recv, g3_send, g3_recv,
    g4_send, g4_recv, local,
):
    e, t, z, x, y, c = place()
    phi = c * NY + y
    half = y // 2
    width = hid.shape[1]
    barrier, count = greet(e, t, z, x)
    started = []

    def normalize():
        values = token_ref[...].astype(F32)
        inv_rms = lax.rsqrt(jnp.mean(values * values, axis=1, keepdims=True) + 1e-06)
        return values, inv_rms, values * inv_rms

    normed_ref[...] = (normalize()[2] * weight_ref[...]).astype(BF)
    probs = probs_ref[...]
    high = probs.astype(BF).astype(F32)
    low = probs - high
    ids = ids_ref[...].astype(F32)
    zbuf[0, :OWN, :TOK] = jnp.concatenate([ids, high], axis=0).astype(BF)
    zbuf[0, :OWN, TOK:] = jnp.concatenate([low, jnp.zeros_like(low)], axis=0).astype(BF)
    pl.semaphore_wait(barrier, count)

    def feat(index):
        return pl.ds(pl.multiple_of(index * FEAT, FEAT), FEAT)

    def core_half(index):
        return pl.ds(pl.multiple_of(index * (NY * FEAT), NY * FEAT), NY * FEAT)

    def block16(index, size):
        return pl.ds(pl.multiple_of(index * size, 16), size)

    def go(src, dst, send, recv, n, device):
        copy = remote(src, dst, send.at[n], recv.at[n], device)
        copy.start()
        started.append(copy)
        return copy

    def others():
        return [(i, lax.rem(t + i, NT)) for i in range(1, NT)]

    def phi_of(other):
        return lax.rem(other, NC) * NY + other // NC

    right = (lax.rem(z + 1, NZ) * NX + x, t)
    left = (lax.rem(z + NZ - 1, NZ) * NX + x, t)

    stays = []
    arrivals = []
    for arr, ref in enumerate((normed_ref, cot_ref)):
        row_at = block16(1 + arr * (TOK // OWN) + t, OWN)
        for i, other in others():
            n = arr * (NT - 1) + i - 1
            arrivals.append(
                go(ref.at[:, feat(phi_of(other))], zbuf.at[0, row_at, :], a_send, a_recv, n, (e, other))
            )
        stay = pltpu.make_async_copy(ref.at[:, feat(phi)], zbuf.at[0, row_at, :], local.at[arr])
        stay.start()
        stays.append(stay)

    pieces = (pl.ds(0, 96), pl.ds(96, 96), pl.ds(192, 80))

    def hop(step, way, p):
        sign = -1 if way == 0 else 1
        src, dst = SLOT_OF[sign * (step - 1)], SLOT_OF[sign * step]
        return go(
            zbuf.at[src, pieces[p], :], zbuf.at[dst, pieces[p], :], z_send, z_recv,
            (way * 8 + step - 1) * len(pieces) + p, right if way == 0 else left,
        )

    def named_experts():
        base = lax.convert_element_type(z * (2 * NX), F32)
        return base + lax.broadcasted_iota(jnp.int32, (8, TOK), 0).astype(F32)

    def build(b):
        named = named_experts()
        chosen, high, low = [], [], []
        for j in range(BATCH):
            meta = zbuf[b * BATCH + j, :OWN, :].astype(F32)
            got, hi, lo = jnp.zeros((8, TOK), F32), jnp.zeros((8, TOK), F32), jnp.zeros((8, TOK), F32)
            for k in range(TOP):
                same = meta[k : k + 1, :TOK] == named
                got = got + jnp.where(same, 1.0, 0.0)
                hi = hi + jnp.where(same, meta[8 + k : 9 + k, :TOK], 0.0)
                lo = lo + jnp.where(same, meta[k : k + 1, TOK:], 0.0)
            chosen.append(got)
            high.append(hi)
            low.append(lo)
        taken = jnp.concatenate(chosen, axis=0)
        rank = jnp.dot(taken.astype(BF), tri_ref[...], preferred_element_type=F32)
        code = jnp.where(taken > 0.5, rank, -1.0)
        codes = jnp.concatenate(
            [
                jnp.concatenate([code[8 * j : 8 * j + 8] for j in range(BATCH)], axis=1),
                jnp.concatenate(high, axis=1),
                jnp.concatenate(low, axis=1),
            ],
            axis=0,
        )
        for f in range(2 * NX):
            hit = codes[f : f + 1, :] == rmat_ref[...]
            rows = pl.ds(f * CHUNK, CHUNK)
            select[b, 0, rows, :] = jnp.where(hit, 1.0, 0.0).astype(BF)
            select[b, 1, rows, :] = jnp.where(hit, codes[8 + f : 9 + f, :], 0.0).astype(BF)
            select[b, 2, rows, :] = jnp.where(hit, codes[16 + f : 17 + f, :], 0.0).astype(BF)

    def stage_x(b):
        these = pl.ds(b * BATCH, BATCH)
        normed = zbuf[these, OWN : OWN + TOK, :].reshape(WIDE, FEAT)
        cot = zbuf[these, OWN + TOK :, :].reshape(WIDE, FEAT)
        picked = jnp.dot(select[b, 0], normed, preferred_element_type=F32).astype(BF)
        grads = (
            jnp.dot(select[b, 1], cot, preferred_element_type=F32)
            + jnp.dot(select[b, 2], cot, preferred_element_type=F32)
        ).astype(BF)
        xs[b, :, :, 0] = picked.reshape(NX, 2, CHUNK, FEAT)
        xs[b, :, :, 1] = grads.reshape(NX, 2, CHUNK, FEAT)
        at = block16(x, CHUNK)
        copies = []
        for i in range(1, NX):
            other = lax.rem(x + i, NX)
            copies.append(
                go(
                    xs.at[b, other], yb.at[b, :, :, at, :], x_send, x_recv,
                    b * (NX - 1) + i - 1, (z * NX + other, t),
                )
            )
        stay = pltpu.make_async_copy(xs.at[b, x], yb.at[b, :, :, at, :], local.at[2 + b])
        stay.start()
        return copies, stay

    def stage_y(b, earlier):
        copies, stay = earlier
        for copy in copies:
            copy.wait_recv()
        stay.wait()
        where = pl.ds(b * ROWS, ROWS)
        sent = []
        for i in range(1, NY):
            other = lax.rem(y + i, NY)
            sent.append(
                go(
                    yb.at[b, other // 2], routed.at[:, where, feat(phi)], y_send, y_recv,
                    b * (NY - 1) + i - 1, (e, other * NC + c),
                )
            )
        keep = pltpu.make_async_copy(yb.at[b, half], routed.at[:, where, feat(phi)], local.at[2 + NB + b])
        keep.start()
        return sent, keep

    def stage_c(b, earlier):
        sent, keep = earlier
        for copy in sent:
            copy.wait_recv()
        keep.wait()
        block = routed.at[:, pl.ds(b * ROWS, ROWS), core_half(c)]
        return go(block, block, c_send, c_recv, b, (e, y * NC + 1 - c))

    def compute(b, earlier):
        earlier.wait_recv()
        where = pl.ds(b * ROWS, ROWS)
        projected = jnp.dot(routed[0, where, :], up_ref[...], preferred_element_type=F32)
        gate_pre, up_pre = projected[:, :width], projected[:, width:]
        sig = jax.nn.sigmoid(gate_pre)
        hidden = (gate_pre * sig * up_pre).astype(BF)
        hid[where, :] = hidden
        hidden_grad = lax.dot_general(routed[1, where, :], down_ref[...], ACROSS, preferred_element_type=F32)
        both = jnp.concatenate(
            [
                hidden_grad * up_pre * sig * (1.0 + gate_pre * (1.0 - sig)),
                hidden_grad * gate_pre * sig,
            ],
            axis=1,
        ).astype(BF)
        joined[where, :] = both
        for n in range(4):
            cols = pl.ds(n * 2 * FEAT, 2 * FEAT)
            parts[0, where, cols] = jnp.dot(hidden, down_ref[:, cols], preferred_element_type=F32).astype(BF)
            parts[1, where, cols] = lax.dot_general(
                both, up_ref[cols, :], ACROSS, preferred_element_type=F32
            ).astype(BF)
        return go(parts.at[:, where, core_half(1 - c)], cb.at[b], c2_send, c2_recv, b, (e, y * NC + 1 - c))

    def weight_grads():
        for n in range(4):
            cols = pl.ds(n * 2 * FEAT, 2 * FEAT)
            down_grad_ref[:, cols] = lax.dot_general(
                hid[...], routed[1, :, cols], OVER, preferred_element_type=F32
            ).astype(BF)
            grad = lax.dot_general(routed[0, :, cols], joined[...], OVER, preferred_element_type=F32)
            up_grad_ref[cols, :] = grad.astype(BF)
            summed = lax.dot_general(
                jnp.ones((8, 2 * width), F32), grad * up_ref[cols, :].astype(F32), ACROSS,
                precision=lax.Precision.HIGHEST, preferred_element_type=F32,
            ) / weight_ref[:, cols]
            gsend[2 * n] = summed[:, :FEAT]
            gsend[2 * n + 1] = summed[:, FEAT:]

    def back_y(b, earlier):
        earlier.wait_recv()
        for k in range(NY):
            mine = parts[:, pl.ds(b * ROWS, ROWS), feat(c * NY + k)]
            theirs = cb[b, :, :, k * FEAT : (k + 1) * FEAT]
            ys[b, k] = (mine.astype(F32) + theirs.astype(F32)).astype(BF)
        sent = []
        for i in range(1, NY):
            other = lax.rem(y + i, NY)
            sent.append(
                go(
                    ys.at[b, other], yr.at[b, i - 1], y2_send, y2_recv,
                    b * (NY - 1) + i - 1, (e, other * NC + c),
                )
            )
        return sent

    def back_x(b, sent):
        for copy in sent:
            copy.wait_recv()
        odd = lax.rem(y, 2)
        partner = 2 * (1 - odd)
        q[b, half] = (ys[b, y].astype(F32) + yr[b, partner].astype(F32)).astype(BF)
        q[b, 1 - half] = (yr[b, 1].astype(F32) + yr[b, 2 * odd].astype(F32)).astype(BF)
        copies = []
        for i in range(1, NX):
            other = lax.rem(x + i, NX)
            copies.append(
                go(
                    q.at[b, :, :, block16(other, CHUNK), :], xb.at[b, x], x2_send, x2_recv,
                    b * (NX - 1) + i - 1, (z * NX + other, t),
                )
            )
        stay = pltpu.make_async_copy(
            q.at[b, :, :, block16(x, CHUNK), :], xb.at[b, x], local.at[2 + 2 * NB + b]
        )
        stay.start()
        return copies, stay

    def spread(b, earlier):
        copies, stay = earlier
        these = pl.ds(b * BATCH, BATCH)
        cot = zbuf[these, OWN + TOK :, :].reshape(WIDE, FEAT)
        cot_slots = jnp.dot(select[b, 0], cot, preferred_element_type=F32)
        for copy in copies:
            copy.wait_recv()
        stay.wait()
        outs = xb[b, :, :, 0].reshape(SLOTS, FEAT)
        grads = xb[b, :, :, 1].reshape(SLOTS, FEAT)
        first = lax.dot_general(select[b, 1], outs, OVER, preferred_element_type=F32)
        first = first + lax.dot_general(select[b, 2], outs, OVER, preferred_element_type=F32)
        second = lax.dot_general(select[b, 0], grads, OVER, preferred_element_type=F32)
        for j in range(BATCH):
            dense[b * BATCH + j, 0] = first[j * TOK : (j + 1) * TOK]
            dense[b * BATCH + j, 1] = second[j * TOK : (j + 1) * TOK]
        value = jnp.sum(cot_slots * outs.astype(F32), axis=1, keepdims=True)
        by_expert = jnp.concatenate(
            [
                jnp.sum(
                    select[b, 0, f * CHUNK : (f + 1) * CHUNK, :].astype(F32)
                    * value[f * CHUNK : (f + 1) * CHUNK],
                    axis=0, keepdims=True,
                )
                for f in range(2 * NX)
            ],
            axis=0,
        )
        named = named_experts()
        for j in range(BATCH):
            ids = zbuf[b * BATCH + j, :OWN, :TOK].astype(F32)
            mine = by_expert[:, j * TOK : (j + 1) * TOK]
            pdense[b * BATCH + j] = jnp.concatenate(
                [
                    jnp.sum(jnp.where(ids[k : k + 1] == named, mine, 0.0), axis=0, keepdims=True)
                    for k in range(TOP)
                ],
                axis=0,
            )

    ring = {}

    def back_hop(step):
        ways = (0, 1) if step < 7 else (0,)
        device = (right, left)
        slot = (SLOT_OF[8 - step], SLOT_OF[-(7 - step)])
        for arr in range(2):
            for part in range(2):
                some = pl.ds(part * (TOK // 2), TOK // 2)
                for way in ways:
                    n = way * 8 + step
                    value = dense[slot[way], arr, some, :]
                    if step > 0:
                        ring[way, step - 1, arr, part].wait_recv()
                        value = value + ring_in[n - 1, arr, some, :].astype(F32)
                    ring_out[n, arr, some, :] = value.astype(BF)
                    ring[way, step, arr, part] = go(
                        ring_out.at[n, arr, some, :], ring_in.at[n, arr, some, :], z2_send, z2_recv,
                        4 * n + 2 * arr + part, device[way],
                    )
        for way in ways:
            n = way * 8 + step
            value = pdense[slot[way]]
            if step > 0:
                ring[way, step - 1, "prob"].wait_recv()
                ring[way, step - 1, "gain"].wait_recv()
                value = value + pring_in[n - 1]
            pring_out[n] = value
            ring[way, step, "prob"] = go(pring_out.at[n], pring_in.at[n], p_send, p_recv, n, device[way])
            origin = lax.rem(z - step + NZ, NZ) if way == 0 else lax.rem(z + step, NZ)
            ring[way, step, "gain"] = go(gz.at[origin], gz.at[origin], g3_send, g3_recv, n, device[way])

    flying = {}
    for p in range(len(pieces)):
        if p < 2:
            for copy in arrivals[p * (NT - 1) : (p + 1) * (NT - 1)]:
                copy.wait_recv()
            stays[p].wait()
        for way in range(2):
            flying[way, p] = hop(1, way, p)
    xdone, ydone, cdone, back = {}, {}, {}, {}
    for step in range(1, 9):
        for p in range(len(pieces)):
            for way in range(2):
                last = 8 if way == 0 else 7
                if step > last:
                    continue
                flying[way, p].wait_recv()
                if step < last:
                    flying[way, p] = hop(step + 1, way, p)
            if p == 0 and step % 2 == 0:
                build(step // 2 - 1)
        b = step // 2 - 1
        if step % 2 == 0:
            xdone[b] = stage_x(b)
            if b >= 2:
                cdone[b - 2] = stage_c(b - 2, ydone[b - 2])
        elif b >= 0:
            ydone[b] = stage_y(b, xdone[b])
    ydone[3] = stage_y(3, xdone[3])
    back[0] = compute(0, cdone[0])
    cdone[2] = stage_c(2, ydone[2])
    back[1] = compute(1, cdone[1])
    back[2] = compute(2, cdone[2])
    cdone[3] = stage_c(3, ydone[3])
    back[3] = compute(3, cdone[3])

    ysent, xsent = {3: back_y(3, back[3])}, {}
    weight_grads()
    ysent[2] = back_y(2, back[2])
    gains = []
    for i, other in others():
        their = phi_of(other)
        gains.append(go(gsend.at[their], gone.at[i], g1_send, g1_recv, i - 1, (e, other)))
    gone[0] = gsend[phi]
    xsent[3] = back_x(3, ysent[3])
    ysent[1] = back_y(1, back[1])
    for copy in gains:
        copy.wait_recv()
    gain_sum = gone[0]
    for i in range(1, NT):
        gain_sum = gain_sum + gone[i]
    gx[x] = gain_sum
    gains = []
    for i in range(1, NX):
        other = lax.rem(x + i, NX)
        gains.append(go(gx.at[x], gx.at[x], g2_send, g2_recv, i - 1, (z * NX + other, t)))
    spread(3, xsent[3])
    for copy in gains:
        copy.wait_recv()
    gz[z] = gx[0] + gx[1] + gx[2] + gx[3]
    back_hop(0)
    xsent[2] = back_x(2, ysent[2])
    ysent[0] = back_y(0, back[0])
    back_hop(1)
    spread(2, xsent[2])
    back_hop(2)
    xsent[1] = back_x(1, ysent[1])
    back_hop(3)
    spread(1, xsent[1])
    back_hop(4)
    xsent[0] = back_x(0, ysent[0])
    back_hop(5)
    spread(0, xsent[0])
    back_hop(6)
    back_hop(7)

    finals = []
    for arr in range(2):
        for part in range(2):
            ring[0, 7, arr, part].wait_recv()
            ring[1, 6, arr, part].wait_recv()
        total[arr] = dense[0, arr] + ring_in[7, arr].astype(F32) + ring_in[8 + 6, arr].astype(F32)
        for i, other in others():
            n = arr * (NT - 1) + i - 1
            finals.append(
                go(
                    total.at[arr, block16(other, OWN), :], out_ref.at[arr, :, feat(phi)],
                    a2_send, a2_recv, n, (e, other),
                )
            )
        stay = pltpu.make_async_copy(
            total.at[arr, block16(t, OWN), :], out_ref.at[arr, :, feat(phi)], local.at[arr]
        )
        stay.start()
        stays.append(stay)
    for way in range(2):
        for kind in ("prob", "gain"):
            ring[way, 7 - way, kind].wait_recv()
    ptotal[...] = pdense[0] + pring_in[7] + pring_in[8 + 6]
    gain_sum = gz[0]
    for n in range(1, NZ):
        gain_sum = gain_sum + gz[n]
    gain_ref[phi] = gain_sum
    for i, other in others():
        finals.append(go(ptotal, pgot.at[i - 1], pa_send, pa_recv, i - 1, (e, other)))
        finals.append(go(gain_ref.at[phi], gain_ref.at[phi], g4_send, g4_recv, i - 1, (e, other)))
    for copy in finals:
        copy.wait_recv()
    for stay in stays[2:]:
        stay.wait()
    prob_sum = ptotal[...]
    for i in range(NT - 1):
        prob_sum = prob_sum + pgot[i]
    prob_tall[...] = jnp.transpose(prob_sum)
    prob_ref[...] = prob_tall[block16(t, OWN), :]
    for n in range(NT):
        gain_out_ref[:, n * FEAT : (n + 1) * FEAT] = gain_ref[n, 0:1, :]
    values, inv_rms, scaled = normalize()
    mixed_ref[...] = (values + out_ref[0]).astype(BF)
    side = out_ref[1] * weight_ref[...]
    token_grad_ref[...] = (
        cot_ref[...].astype(F32)
        + inv_rms * (side - scaled * jnp.mean(side * scaled, axis=1, keepdims=True))
    ).astype(BF)
    for copy in started:
        copy.wait_send()


def vmem():
    return pl.BlockSpec(memory_space=pltpu.VMEM)


def dma(*counts):
    return [pltpu.SemaphoreType.DMA((n,)) for n in counts for _ in range(2)]


def constants():
    lane = np.arange(WIDE)
    row = np.arange(CHUNK)
    rmat = np.where(lane[None, :] // TOK == row[:, None] // CAP, row[:, None] % CAP, -5)
    tri = np.arange(TOK)[:, None] < np.arange(TOK)[None, :]
    return jnp.asarray(rmat, F32), jnp.asarray(tri, BF)


def experts(tokens, cotangent, gain, expert_ids, gate_probs, gate_up, down_proj):
    features, hidden = NT * FEAT, down_proj.shape[0]
    rows = NB * ROWS
    shape = jax.ShapeDtypeStruct
    rmat, tri = constants()
    return pl.pallas_call(
        experts_kernel,
        out_shape=(
            shape((OWN, features), BF),
            shape((OWN, features), BF),
            shape((OWN, TOP), F32),
            shape((1, features), F32),
            shape((features, 2 * hidden), BF),
            shape((hidden, features), BF),
        ),
        in_specs=[vmem()] * 9,
        out_specs=tuple([vmem()] * 6),
        scratch_shapes=[
            pltpu.VMEM((OWN, features), BF),
            pltpu.VMEM((2, OWN, features), F32),
            pltpu.VMEM((NT, 8, FEAT), F32),
            pltpu.VMEM((TOK, TOP), F32),
            pltpu.VMEM((NZ, 2 * TOK + OWN, FEAT), BF),
            pltpu.VMEM((NB, NX, 2, 2, CHUNK, FEAT), BF),
            pltpu.VMEM((NB, 2, 2, ROWS, FEAT), BF),
            pltpu.VMEM((NB, 3, SLOTS, WIDE), BF),
            pltpu.VMEM((2, rows, features), BF),
            pltpu.VMEM((2, rows, features), BF),
            pltpu.VMEM((rows, hidden), BF),
            pltpu.VMEM((rows, 2 * hidden), BF),
            pltpu.VMEM((NB, 2, ROWS, NY * FEAT), BF),
            pltpu.VMEM((NB, NY, 2, ROWS, FEAT), BF),
            pltpu.VMEM((NB, NY - 1, 2, ROWS, FEAT), BF),
            pltpu.VMEM((NB, 2, 2, ROWS, FEAT), BF),
            pltpu.VMEM((NB, NX, 2, 2, CHUNK, FEAT), BF),
            pltpu.VMEM((NZ, 2, TOK, FEAT), F32),
            pltpu.VMEM((NZ, 2, TOK, FEAT), BF),
            pltpu.VMEM((NZ, 2, TOK, FEAT), BF),
            pltpu.VMEM((2, TOK, FEAT), F32),
            pltpu.VMEM((NZ, TOP, TOK), F32),
            pltpu.VMEM((NZ, TOP, TOK), F32),
            pltpu.VMEM((NZ, TOP, TOK), F32),
            pltpu.VMEM((TOP, TOK), F32),
            pltpu.VMEM((NT - 1, TOP, TOK), F32),
            pltpu.VMEM((NT, 8, FEAT), F32),
            pltpu.VMEM((NT, 8, FEAT), F32),
            pltpu.VMEM((NX, 8, FEAT), F32),
            pltpu.VMEM((NZ, 8, FEAT), F32),
            *dma(2 * (NT - 1), 48, NB * (NX - 1), NB * (NY - 1), NB),
            *dma(NB, NB * (NY - 1), NB * (NX - 1), 64, 2 * (NT - 1)),
            *dma(16, NT - 1, NT - 1, NX - 1, 16, NT - 1),
            pltpu.SemaphoreType.DMA((2 + 3 * NB,)),
        ],
        compiler_params=pltpu.CompilerParams(
            collective_id=0, has_side_effects=True, vmem_limit_bytes=60 * 2**20
        ),
        name="experts",
    )(tokens, cotangent, gain, expert_ids, gate_probs, rmat, tri, gate_up, down_proj)


def shards(tokens, cotangent, gain, expert_ids, gate_probs, gate_up_weight, down_weight):
    mixed, token_grad, prob_grad, gain_grad, gate_up_grad, down_grad = experts(
        tokens, cotangent, gain[None], expert_ids.T, gate_probs.T, gate_up_weight[0], down_weight[0]
    )
    return (mixed, token_grad, prob_grad, gain_grad[0], gate_up_grad[None], down_grad[None])


def solution(mesh):
    both = P(("expert", "tensor"), None)
    cube = P(("expert", "tensor"), None, None)
    in_specs = (both, both, P(), P("expert", None), P("expert", None), cube, cube)
    out_specs = (both, both, both, P(), cube, cube)
    return jax.shard_map(shards, mesh=mesh, in_specs=in_specs, out_specs=out_specs, check_vma=False)
```

```python
import jax
import jax.numpy as jnp
import numpy as np
from jax import lax
from jax.experimental import pallas as pl
from jax.experimental.pallas import tpu as pltpu
from jax.sharding import PartitionSpec as P

TOP = 8
NZ, NX, NY, NC = 16, 4, 4, 2
NT = NY * NC
TOK = 128
OWN = 16
CAP = 12
FEAT = 256
BATCH = 4
NB = NZ // BATCH
CHUNK = BATCH * CAP
ROWS = NX * CHUNK
SLOTS = NX * 2 * CHUNK
WIDE = BATCH * TOK
ORDER = [0, 1, -1, 2, -2, 3, -3, 4, -4, 5, -5, 6, -6, 7, -7, 8]
SLOT_OF = {d: s for s, d in enumerate(ORDER)}
SLOT_OF[-8] = SLOT_OF[8]
BF, F32 = jnp.bfloat16, jnp.float32
ACROSS = (((1,), (1,)), ((), ()))
OVER = (((0,), (0,)), ((), ()))


def place():
    e, t = lax.axis_index("expert"), lax.axis_index("tensor")
    return e, t, e // NX, lax.rem(e, NX), t // NC, lax.rem(t, NC)


def remote(src, dst, send, recv, device):
    return pltpu.make_async_remote_copy(
        src_ref=src, dst_ref=dst, send_sem=send, recv_sem=recv,
        device_id=device, device_id_type=pl.DeviceIdType.MESH,
    )


def greet(e, t, z, x):
    barrier = pltpu.get_barrier_semaphore()
    peers = [(e, lax.rem(t + i, NT)) for i in range(1, NT)]
    peers += [(z * NX + lax.rem(x + i, NX), t) for i in range(1, NX)]
    peers += [(lax.rem(z + i, NZ) * NX + x, t) for i in (1, NZ - 1)]
    for peer in peers:
        pl.semaphore_signal(barrier, inc=1, device_id=peer, device_id_type=pl.DeviceIdType.MESH)
    return barrier, len(peers)


def experts_kernel(
    token_ref, cot_ref, weight_ref, ids_ref, probs_ref, rmat_ref, tri_ref, up_ref, down_ref,
    mixed_ref, token_grad_ref, prob_ref, gain_out_ref, up_grad_ref, down_grad_ref,
    normed_ref, out_ref, gain_ref, prob_tall,
    zbuf, xs, yb, select, routed, parts, hid, joined,
    cb, ys, yr, q, xb, dense, ring_out, ring_in, total,
    pdense, pring_out, pring_in, ptotal, pgot, gsend, gone, gx, gz,
    a_send, a_recv, z_send, z_recv, x_send, x_recv, y_send, y_recv, c_send, c_recv,
    c2_send, c2_recv, y2_send, y2_recv, x2_send, x2_recv, z2_send, z2_recv, a2_send, a2_recv,
    p_send, p_recv, pa_send, pa_recv, g1_send, g1_recv, g2_send, g2_recv, g3_send, g3_recv,
    g4_send, g4_recv, local,
):
    e, t, z, x, y, c = place()
    phi = c * NY + y
    half = y // 2
    width = hid.shape[1]
    barrier, count = greet(e, t, z, x)
    started = []

    def normalize():
        values = token_ref[...].astype(F32)
        inv_rms = lax.rsqrt(jnp.mean(values * values, axis=1, keepdims=True) + 1e-06)
        return values, inv_rms, values * inv_rms

    normed_ref[...] = (normalize()[2] * weight_ref[...]).astype(BF)
    probs = probs_ref[...]
    high = probs.astype(BF).astype(F32)
    low = probs - high
    ids = ids_ref[...].astype(F32)
    zbuf[0, :OWN, :TOK] = jnp.concatenate([ids, high], axis=0).astype(BF)
    zbuf[0, :OWN, TOK:] = jnp.concatenate([low, jnp.zeros_like(low)], axis=0).astype(BF)
    pl.semaphore_wait(barrier, count)

    def feat(index):
        return pl.ds(pl.multiple_of(index * FEAT, FEAT), FEAT)

    def core_half(index):
        return pl.ds(pl.multiple_of(index * (NY * FEAT), NY * FEAT), NY * FEAT)

    def block16(index, size):
        return pl.ds(pl.multiple_of(index * size, 16), size)

    def go(src, dst, send, recv, n, device):
        copy = remote(src, dst, send.at[n], recv.at[n], device)
        copy.start()
        started.append(copy)
        return copy

    def others():
        return [(i, lax.rem(t + i, NT)) for i in range(1, NT)]

    def phi_of(other):
        return lax.rem(other, NC) * NY + other // NC

    right = (lax.rem(z + 1, NZ) * NX + x, t)
    left = (lax.rem(z + NZ - 1, NZ) * NX + x, t)

    stays = []
    arrivals = []
    for arr, ref in enumerate((normed_ref, cot_ref)):
        row_at = block16(1 + arr * (TOK // OWN) + t, OWN)
        for i, other in others():
            n = arr * (NT - 1) + i - 1
            arrivals.append(
                go(ref.at[:, feat(phi_of(other))], zbuf.at[0, row_at, :], a_send, a_recv, n, (e, other))
            )
        stay = pltpu.make_async_copy(ref.at[:, feat(phi)], zbuf.at[0, row_at, :], local.at[arr])
        stay.start()
        stays.append(stay)

    pieces = (pl.ds(0, 96), pl.ds(96, 96), pl.ds(192, 80))

    def hop(step, way, p):
        sign = -1 if way == 0 else 1
        src, dst = SLOT_OF[sign * (step - 1)], SLOT_OF[sign * step]
        return go(
            zbuf.at[src, pieces[p], :], zbuf.at[dst, pieces[p], :], z_send, z_recv,
            (way * 8 + step - 1) * len(pieces) + p, right if way == 0 else left,
        )

    def named_experts():
        base = lax.convert_element_type(z * (2 * NX), F32)
        return base + lax.broadcasted_iota(jnp.int32, (8, TOK), 0).astype(F32)

    def build(b):
        named = named_experts()
        chosen, high, low = [], [], []
        for j in range(BATCH):
            meta = zbuf[b * BATCH + j, :OWN, :].astype(F32)
            got, hi, lo = jnp.zeros((8, TOK), F32), jnp.zeros((8, TOK), F32), jnp.zeros((8, TOK), F32)
            for k in range(TOP):
                same = meta[k : k + 1, :TOK] == named
                got = got + jnp.where(same, 1.0, 0.0)
                hi = hi + jnp.where(same, meta[8 + k : 9 + k, :TOK], 0.0)
                lo = lo + jnp.where(same, meta[k : k + 1, TOK:], 0.0)
            chosen.append(got)
            high.append(hi)
            low.append(lo)
        taken = jnp.concatenate(chosen, axis=0)
        rank = jnp.dot(taken.astype(BF), tri_ref[...], preferred_element_type=F32)
        code = jnp.where(taken > 0.5, rank, -1.0)
        codes = jnp.concatenate(
            [
                jnp.concatenate([code[8 * j : 8 * j + 8] for j in range(BATCH)], axis=1),
                jnp.concatenate(high, axis=1),
                jnp.concatenate(low, axis=1),
            ],
            axis=0,
        )
        for f in range(2 * NX):
            hit = codes[f : f + 1, :] == rmat_ref[...]
            rows = pl.ds(f * CHUNK, CHUNK)
            select[b, 0, rows, :] = jnp.where(hit, 1.0, 0.0).astype(BF)
            select[b, 1, rows, :] = jnp.where(hit, codes[8 + f : 9 + f, :], 0.0).astype(BF)
            select[b, 2, rows, :] = jnp.where(hit, codes[16 + f : 17 + f, :], 0.0).astype(BF)

    def stage_x(b):
        these = pl.ds(b * BATCH, BATCH)
        normed = zbuf[these, OWN : OWN + TOK, :].reshape(WIDE, FEAT)
        cot = zbuf[these, OWN + TOK :, :].reshape(WIDE, FEAT)
        picked = jnp.dot(select[b, 0], normed, preferred_element_type=F32).astype(BF)
        grads = (
            jnp.dot(select[b, 1], cot, preferred_element_type=F32)
            + jnp.dot(select[b, 2], cot, preferred_element_type=F32)
        ).astype(BF)
        xs[b, :, :, 0] = picked.reshape(NX, 2, CHUNK, FEAT)
        xs[b, :, :, 1] = grads.reshape(NX, 2, CHUNK, FEAT)
        at = block16(x, CHUNK)
        copies = []
        for i in range(1, NX):
            other = lax.rem(x + i, NX)
            copies.append(
                go(
                    xs.at[b, other], yb.at[b, :, :, at, :], x_send, x_recv,
                    b * (NX - 1) + i - 1, (z * NX + other, t),
                )
            )
        stay = pltpu.make_async_copy(xs.at[b, x], yb.at[b, :, :, at, :], local.at[2 + b])
        stay.start()
        return copies, stay

    def stage_y(b, earlier):
        copies, stay = earlier
        for copy in copies:
            copy.wait_recv()
        stay.wait()
        where = pl.ds(b * ROWS, ROWS)
        sent = []
        for i in range(1, NY):
            other = lax.rem(y + i, NY)
            sent.append(
                go(
                    yb.at[b, other // 2], routed.at[:, where, feat(phi)], y_send, y_recv,
                    b * (NY - 1) + i - 1, (e, other * NC + c),
                )
            )
        keep = pltpu.make_async_copy(yb.at[b, half], routed.at[:, where, feat(phi)], local.at[2 + NB + b])
        keep.start()
        return sent, keep

    def stage_c(b, earlier):
        sent, keep = earlier
        for copy in sent:
            copy.wait_recv()
        keep.wait()
        block = routed.at[:, pl.ds(b * ROWS, ROWS), core_half(c)]
        return go(block, block, c_send, c_recv, b, (e, y * NC + 1 - c))

    def compute(b, earlier):
        earlier.wait_recv()
        where = pl.ds(b * ROWS, ROWS)
        projected = jnp.dot(routed[0, where, :], up_ref[...], preferred_element_type=F32)
        gate_pre, up_pre = projected[:, :width], projected[:, width:]
        sig = jax.nn.sigmoid(gate_pre)
        hidden = (gate_pre * sig * up_pre).astype(BF)
        hid[where, :] = hidden
        hidden_grad = lax.dot_general(routed[1, where, :], down_ref[...], ACROSS, preferred_element_type=F32)
        both = jnp.concatenate(
            [
                hidden_grad * up_pre * sig * (1.0 + gate_pre * (1.0 - sig)),
                hidden_grad * gate_pre * sig,
            ],
            axis=1,
        ).astype(BF)
        joined[where, :] = both
        for n in range(4):
            cols = pl.ds(n * 2 * FEAT, 2 * FEAT)
            parts[0, where, cols] = jnp.dot(hidden, down_ref[:, cols], preferred_element_type=F32).astype(BF)
            parts[1, where, cols] = lax.dot_general(
                both, up_ref[cols, :], ACROSS, preferred_element_type=F32
            ).astype(BF)
        return go(parts.at[:, where, core_half(1 - c)], cb.at[b], c2_send, c2_recv, b, (e, y * NC + 1 - c))

    def down_grads(n):
        cols = pl.ds(n * 2 * FEAT, 2 * FEAT)
        down_grad_ref[:, cols] = lax.dot_general(
            hid[...], routed[1, :, cols], OVER, preferred_element_type=F32
        ).astype(BF)

    def up_grads():
        for n in range(4):
            cols = pl.ds(n * 2 * FEAT, 2 * FEAT)
            grad = lax.dot_general(routed[0, :, cols], joined[...], OVER, preferred_element_type=F32)
            up_grad_ref[cols, :] = grad.astype(BF)
            summed = lax.dot_general(
                jnp.ones((8, 2 * width), F32), grad * up_ref[cols, :].astype(F32), ACROSS,
                precision=lax.Precision.HIGHEST, preferred_element_type=F32,
            ) / weight_ref[:, cols]
            gsend[2 * n] = summed[:, :FEAT]
            gsend[2 * n + 1] = summed[:, FEAT:]

    def back_y(b, earlier):
        earlier.wait_recv()
        for k in range(NY):
            mine = parts[:, pl.ds(b * ROWS, ROWS), feat(c * NY + k)]
            theirs = cb[b, :, :, k * FEAT : (k + 1) * FEAT]
            ys[b, k] = (mine.astype(F32) + theirs.astype(F32)).astype(BF)
        sent = []
        for i in range(1, NY):
            other = lax.rem(y + i, NY)
            sent.append(
                go(
                    ys.at[b, other], yr.at[b, i - 1], y2_send, y2_recv,
                    b * (NY - 1) + i - 1, (e, other * NC + c),
                )
            )
        return sent

    def back_x(b, sent):
        for copy in sent:
            copy.wait_recv()
        odd = lax.rem(y, 2)
        partner = 2 * (1 - odd)
        q[b, half] = (ys[b, y].astype(F32) + yr[b, partner].astype(F32)).astype(BF)
        q[b, 1 - half] = (yr[b, 1].astype(F32) + yr[b, 2 * odd].astype(F32)).astype(BF)
        copies = []
        for i in range(1, NX):
            other = lax.rem(x + i, NX)
            copies.append(
                go(
                    q.at[b, :, :, block16(other, CHUNK), :], xb.at[b, x], x2_send, x2_recv,
                    b * (NX - 1) + i - 1, (z * NX + other, t),
                )
            )
        stay = pltpu.make_async_copy(
            q.at[b, :, :, block16(x, CHUNK), :], xb.at[b, x], local.at[2 + 2 * NB + b]
        )
        stay.start()
        return copies, stay

    def spread(b, earlier):
        copies, stay = earlier
        these = pl.ds(b * BATCH, BATCH)
        cot = zbuf[these, OWN + TOK :, :].reshape(WIDE, FEAT)
        cot_slots = jnp.dot(select[b, 0], cot, preferred_element_type=F32)
        for copy in copies:
            copy.wait_recv()
        stay.wait()
        outs = xb[b, :, :, 0].reshape(SLOTS, FEAT)
        grads = xb[b, :, :, 1].reshape(SLOTS, FEAT)
        first = lax.dot_general(select[b, 1], outs, OVER, preferred_element_type=F32)
        first = first + lax.dot_general(select[b, 2], outs, OVER, preferred_element_type=F32)
        second = lax.dot_general(select[b, 0], grads, OVER, preferred_element_type=F32)
        for j in range(BATCH):
            dense[b * BATCH + j, 0] = first[j * TOK : (j + 1) * TOK]
            dense[b * BATCH + j, 1] = second[j * TOK : (j + 1) * TOK]
        value = jnp.sum(cot_slots * outs.astype(F32), axis=1, keepdims=True)
        by_expert = jnp.concatenate(
            [
                jnp.sum(
                    select[b, 0, f * CHUNK : (f + 1) * CHUNK, :].astype(F32)
                    * value[f * CHUNK : (f + 1) * CHUNK],
                    axis=0, keepdims=True,
                )
                for f in range(2 * NX)
            ],
            axis=0,
        )
        named = named_experts()
        for j in range(BATCH):
            ids = zbuf[b * BATCH + j, :OWN, :TOK].astype(F32)
            mine = by_expert[:, j * TOK : (j + 1) * TOK]
            pdense[b * BATCH + j] = jnp.concatenate(
                [
                    jnp.sum(jnp.where(ids[k : k + 1] == named, mine, 0.0), axis=0, keepdims=True)
                    for k in range(TOP)
                ],
                axis=0,
            )

    ring = {}

    def back_hop(step):
        ways = (0, 1) if step < 7 else (0,)
        device = (right, left)
        slot = (SLOT_OF[8 - step], SLOT_OF[-(7 - step)])
        for arr in range(2):
            for part in range(2):
                some = pl.ds(part * (TOK // 2), TOK // 2)
                for way in ways:
                    n = way * 8 + step
                    value = dense[slot[way], arr, some, :]
                    if step > 0:
                        ring[way, step - 1, arr, part].wait_recv()
                        value = value + ring_in[n - 1, arr, some, :].astype(F32)
                    ring_out[n, arr, some, :] = value.astype(BF)
                    ring[way, step, arr, part] = go(
                        ring_out.at[n, arr, some, :], ring_in.at[n, arr, some, :], z2_send, z2_recv,
                        4 * n + 2 * arr + part, device[way],
                    )
        for way in ways:
            n = way * 8 + step
            value = pdense[slot[way]]
            if step > 0:
                ring[way, step - 1, "prob"].wait_recv()
                ring[way, step - 1, "gain"].wait_recv()
                value = value + pring_in[n - 1]
            pring_out[n] = value
            ring[way, step, "prob"] = go(pring_out.at[n], pring_in.at[n], p_send, p_recv, n, device[way])
            origin = lax.rem(z - step + NZ, NZ) if way == 0 else lax.rem(z + step, NZ)
            ring[way, step, "gain"] = go(gz.at[origin], gz.at[origin], g3_send, g3_recv, n, device[way])

    flying = {}
    for p in range(len(pieces)):
        if p < 2:
            for copy in arrivals[p * (NT - 1) : (p + 1) * (NT - 1)]:
                copy.wait_recv()
            stays[p].wait()
        for way in range(2):
            flying[way, p] = hop(1, way, p)
    xdone, ydone, cdone, back = {}, {}, {}, {}
    for step in range(1, 9):
        for p in range(len(pieces)):
            for way in range(2):
                last = 8 if way == 0 else 7
                if step > last:
                    continue
                flying[way, p].wait_recv()
                if step < last:
                    flying[way, p] = hop(step + 1, way, p)
            if p == 0 and step % 2 == 0:
                build(step // 2 - 1)
        b = step // 2 - 1
        if step % 2 == 0:
            xdone[b] = stage_x(b)
            if b >= 2:
                cdone[b - 2] = stage_c(b - 2, ydone[b - 2])
        elif b >= 0:
            ydone[b] = stage_y(b, xdone[b])
    ydone[3] = stage_y(3, xdone[3])
    back[0] = compute(0, cdone[0])
    cdone[2] = stage_c(2, ydone[2])
    back[1] = compute(1, cdone[1])
    back[2] = compute(2, cdone[2])
    cdone[3] = stage_c(3, ydone[3])
    back[3] = compute(3, cdone[3])

    ysent, xsent = {3: back_y(3, back[3])}, {}
    up_grads()
    ysent[2] = back_y(2, back[2])
    gains = []
    for i, other in others():
        their = phi_of(other)
        gains.append(go(gsend.at[their], gone.at[i], g1_send, g1_recv, i - 1, (e, other)))
    gone[0] = gsend[phi]
    xsent[3] = back_x(3, ysent[3])
    ysent[1] = back_y(1, back[1])
    for copy in gains:
        copy.wait_recv()
    gain_sum = gone[0]
    for i in range(1, NT):
        gain_sum = gain_sum + gone[i]
    gx[x] = gain_sum
    gains = []
    for i in range(1, NX):
        other = lax.rem(x + i, NX)
        gains.append(go(gx.at[x], gx.at[x], g2_send, g2_recv, i - 1, (z * NX + other, t)))
    spread(3, xsent[3])
    for copy in gains:
        copy.wait_recv()
    gz[z] = gx[0] + gx[1] + gx[2] + gx[3]
    back_hop(0)
    xsent[2] = back_x(2, ysent[2])
    ysent[0] = back_y(0, back[0])
    back_hop(1)
    down_grads(0)
    spread(2, xsent[2])
    back_hop(2)
    xsent[1] = back_x(1, ysent[1])
    back_hop(3)
    down_grads(1)
    spread(1, xsent[1])
    back_hop(4)
    xsent[0] = back_x(0, ysent[0])
    back_hop(5)
    down_grads(2)
    spread(0, xsent[0])
    back_hop(6)
    down_grads(3)
    back_hop(7)

    finals = []
    for arr in range(2):
        for part in range(2):
            ring[0, 7, arr, part].wait_recv()
            ring[1, 6, arr, part].wait_recv()
        total[arr] = dense[0, arr] + ring_in[7, arr].astype(F32) + ring_in[8 + 6, arr].astype(F32)
        for i, other in others():
            n = arr * (NT - 1) + i - 1
            finals.append(
                go(
                    total.at[arr, block16(other, OWN), :], out_ref.at[arr, :, feat(phi)],
                    a2_send, a2_recv, n, (e, other),
                )
            )
        stay = pltpu.make_async_copy(
            total.at[arr, block16(t, OWN), :], out_ref.at[arr, :, feat(phi)], local.at[arr]
        )
        stay.start()
        stays.append(stay)
    for way in range(2):
        for kind in ("prob", "gain"):
            ring[way, 7 - way, kind].wait_recv()
    ptotal[...] = pdense[0] + pring_in[7] + pring_in[8 + 6]
    gain_sum = gz[0]
    for n in range(1, NZ):
        gain_sum = gain_sum + gz[n]
    gain_ref[phi] = gain_sum
    for i, other in others():
        finals.append(go(ptotal, pgot.at[i - 1], pa_send, pa_recv, i - 1, (e, other)))
        finals.append(go(gain_ref.at[phi], gain_ref.at[phi], g4_send, g4_recv, i - 1, (e, other)))
    for copy in finals:
        copy.wait_recv()
    for stay in stays[2:]:
        stay.wait()
    prob_sum = ptotal[...]
    for i in range(NT - 1):
        prob_sum = prob_sum + pgot[i]
    prob_tall[...] = jnp.transpose(prob_sum)
    prob_ref[...] = prob_tall[block16(t, OWN), :]
    for n in range(NT):
        gain_out_ref[:, n * FEAT : (n + 1) * FEAT] = gain_ref[n, 0:1, :]
    values, inv_rms, scaled = normalize()
    mixed_ref[...] = (values + out_ref[0]).astype(BF)
    side = out_ref[1] * weight_ref[...]
    token_grad_ref[...] = (
        cot_ref[...].astype(F32)
        + inv_rms * (side - scaled * jnp.mean(side * scaled, axis=1, keepdims=True))
    ).astype(BF)
    for copy in started:
        copy.wait_send()


def vmem():
    return pl.BlockSpec(memory_space=pltpu.VMEM)


def dma(*counts):
    return [pltpu.SemaphoreType.DMA((n,)) for n in counts for _ in range(2)]


def constants():
    lane = np.arange(WIDE)
    row = np.arange(CHUNK)
    rmat = np.where(lane[None, :] // TOK == row[:, None] // CAP, row[:, None] % CAP, -5)
    tri = np.arange(TOK)[:, None] < np.arange(TOK)[None, :]
    return jnp.asarray(rmat, F32), jnp.asarray(tri, BF)


def experts(tokens, cotangent, gain, expert_ids, gate_probs, gate_up, down_proj):
    features, hidden = NT * FEAT, down_proj.shape[0]
    rows = NB * ROWS
    shape = jax.ShapeDtypeStruct
    rmat, tri = constants()
    return pl.pallas_call(
        experts_kernel,
        out_shape=(
            shape((OWN, features), BF),
            shape((OWN, features), BF),
            shape((OWN, TOP), F32),
            shape((1, features), F32),
            shape((features, 2 * hidden), BF),
            shape((hidden, features), BF),
        ),
        in_specs=[vmem()] * 9,
        out_specs=tuple([vmem()] * 6),
        scratch_shapes=[
            pltpu.VMEM((OWN, features), BF),
            pltpu.VMEM((2, OWN, features), F32),
            pltpu.VMEM((NT, 8, FEAT), F32),
            pltpu.VMEM((TOK, TOP), F32),
            pltpu.VMEM((NZ, 2 * TOK + OWN, FEAT), BF),
            pltpu.VMEM((NB, NX, 2, 2, CHUNK, FEAT), BF),
            pltpu.VMEM((NB, 2, 2, ROWS, FEAT), BF),
            pltpu.VMEM((NB, 3, SLOTS, WIDE), BF),
            pltpu.VMEM((2, rows, features), BF),
            pltpu.VMEM((2, rows, features), BF),
            pltpu.VMEM((rows, hidden), BF),
            pltpu.VMEM((rows, 2 * hidden), BF),
            pltpu.VMEM((NB, 2, ROWS, NY * FEAT), BF),
            pltpu.VMEM((NB, NY, 2, ROWS, FEAT), BF),
            pltpu.VMEM((NB, NY - 1, 2, ROWS, FEAT), BF),
            pltpu.VMEM((NB, 2, 2, ROWS, FEAT), BF),
            pltpu.VMEM((NB, NX, 2, 2, CHUNK, FEAT), BF),
            pltpu.VMEM((NZ, 2, TOK, FEAT), F32),
            pltpu.VMEM((NZ, 2, TOK, FEAT), BF),
            pltpu.VMEM((NZ, 2, TOK, FEAT), BF),
            pltpu.VMEM((2, TOK, FEAT), F32),
            pltpu.VMEM((NZ, TOP, TOK), F32),
            pltpu.VMEM((NZ, TOP, TOK), F32),
            pltpu.VMEM((NZ, TOP, TOK), F32),
            pltpu.VMEM((TOP, TOK), F32),
            pltpu.VMEM((NT - 1, TOP, TOK), F32),
            pltpu.VMEM((NT, 8, FEAT), F32),
            pltpu.VMEM((NT, 8, FEAT), F32),
            pltpu.VMEM((NX, 8, FEAT), F32),
            pltpu.VMEM((NZ, 8, FEAT), F32),
            *dma(2 * (NT - 1), 48, NB * (NX - 1), NB * (NY - 1), NB),
            *dma(NB, NB * (NY - 1), NB * (NX - 1), 64, 2 * (NT - 1)),
            *dma(16, NT - 1, NT - 1, NX - 1, 16, NT - 1),
            pltpu.SemaphoreType.DMA((2 + 3 * NB,)),
        ],
        compiler_params=pltpu.CompilerParams(
            collective_id=0, has_side_effects=True, vmem_limit_bytes=60 * 2**20
        ),
        name="experts",
    )(tokens, cotangent, gain, expert_ids, gate_probs, rmat, tri, gate_up, down_proj)


def shards(tokens, cotangent, gain, expert_ids, gate_probs, gate_up_weight, down_weight):
    mixed, token_grad, prob_grad, gain_grad, gate_up_grad, down_grad = experts(
        tokens, cotangent, gain[None], expert_ids.T, gate_probs.T, gate_up_weight[0], down_weight[0]
    )
    return (mixed, token_grad, prob_grad, gain_grad[0], gate_up_grad[None], down_grad[None])


def solution(mesh):
    both = P(("expert", "tensor"), None)
    cube = P(("expert", "tensor"), None, None)
    in_specs = (both, both, P(), P("expert", None), P("expert", None), cube, cube)
    out_specs = (both, both, both, P(), cube, cube)
    return jax.shard_map(shards, mesh=mesh, in_specs=in_specs, out_specs=out_specs, check_vma=False)
```
